512 devices in a mesh: step: 8 (over y, core), node: 2 (over x_lo), space: 32 (over x_hi, z).
Axes of the slice: x: 4 (x_hi: 2, x_lo: 2; x = x_hi * 2 + x_lo), y: 4, z: 16, core: 2. Of those that a mesh axis runs over, the one named last changes fastest.
Arguments:
- iterate: float32 [16, 4, 64, 32, 256], P('step', 'node', 'space'), may hold values from -2.5 to 2.5
- initial_value: float32 [64, 32, 256], P('space'), may hold values from -2.5 to 2.5
- alpha_power: int32 [1], replicated, may hold values from 8 to 72
- node_mix: float32 [2, 16, 4, 4], P(None, 'step', 'node'), may hold values from -0.4 to 1.4
- node_back: float32 [2, 16, 4, 4], P(None, 'step', 'node'), may hold values from -0.4 to 1.4
- shifts: float32 [2, 16, 4], P(None, 'step', 'node'), may hold values from -0.4 to 0.8, as said below
Outputs:
- updated: float32 [16, 4, 64, 32, 256], P('step', 'node', 'space')
- new_residual: float32 [16, 4, 64, 32, 256], P('step', 'node', 'space')
The draws below stay inside these ranges and needn't reach their ends.
Inputs may be any that keep to these rules, and one draw needn't show every extreme that they name: shifts[0] lies in 0.2 to 0.8, shifts[1] in -0.4 to 0.4.
All inputs are finite; a program needn't handle non-finite values.
Results may differ from the reference program's by a relative error of at most 0.0003.
Values sent between devices are 32-bit elements; how exact they have to be, the bound alone decides.
A program may use at most 64 MiB of HBM per device.

```python
import math
import jax
import jax.numpy as jnp
from jax import lax

STEPS = 16
NODES = 4
SWEEPS = 8
GX = 32
GY = 256
NZ = 64


def mixing_matrix(key, spread, bend_power):
    array_shape = (2, STEPS, NODES, NODES)
    uniform_part = jax.random.uniform(key, array_shape, jnp.float32, -1.0, 1.0)
    values = spread * jnp.sign(uniform_part) * jnp.abs(uniform_part) ** bend_power
    row_index = lax.broadcasted_iota(jnp.int32, array_shape, 2)
    col_index = lax.broadcasted_iota(jnp.int32, array_shape, 3)
    component = lax.broadcasted_iota(jnp.int32, array_shape, 0)
    identity = ((row_index == col_index) & (component == 0)).astype(jnp.float32)
    return identity + values


def draw_node_mix(key, part):
    key = jax.random.fold_in(key, 12)
    bend_power = 1.0
    return mixing_matrix(key, 0.4, bend_power)


def draw_node_back(key, part):
    key = jax.random.fold_in(key, 13)
    bend_power = 1.0
    return mixing_matrix(key, 0.4, bend_power)


def draw_shifts(key, part):
    key = jax.random.fold_in(key, 11)
    key_real, key_imag = jax.random.split(key)
    bend_power = 1.0
    unit_re = jax.random.uniform(key_real, (1, STEPS, NODES), jnp.float32, 0.0, 1.0)
    unit_im = jax.random.uniform(key_imag, (1, STEPS, NODES), jnp.float32, -1.0, 1.0)
    real_part = 0.2 + 0.6 * unit_re ** bend_power
    imag_part = 0.4 * jnp.sign(unit_im) * jnp.abs(unit_im) ** bend_power
    return jnp.concatenate([real_part, imag_part], 0)


def steps_of(own_key, shape, pieces, least, high):
    def one(dim, blocks):
        steps = jax.random.uniform(jax.random.fold_in(jax.random.fold_in(own_key, 6), dim), (blocks,), jnp.float32, least / len(pieces), high / len(pieces))
        return jnp.repeat(jnp.exp(steps), shape[dim] // blocks).reshape((-1,) + (1,) * (len(shape) - dim - 1))

    gain = one(*pieces[0])
    for cut in pieces[1:]:
        gain = gain * one(*cut)
    return gain


def gaussian(own_key, dims, scale, reach, cuts=(), kind=jnp.bfloat16):
    level = steps_of(own_key, dims, cuts, -0.22, 0.18) if cuts else 1.0
    result = jax.random.normal(own_key, dims, jnp.float32) * scale * level
    return jnp.minimum(jnp.maximum(result, -reach), reach).astype(kind)


def setup_inputs(seed: int = 0) -> dict:
    key_of = jax.random.split(jax.random.key(seed), 7)
    return {
        "iterate": gaussian(key_of[0], (STEPS, NODES, NZ, GX, GY), 0.5, 2.5, ((0, 8), (1, 2), (2, 32)), jnp.float32),
        "initial_value": gaussian(key_of[1], (NZ, GX, GY), 0.5, 2.5, ((0, 32),), jnp.float32),
        "alpha_power": jax.random.randint(key_of[2], (1,), 8, 73).astype(jnp.int32),
        "node_mix": draw_node_mix(jax.random.fold_in(key_of[6], 71), 0),
        "node_back": draw_node_back(jax.random.fold_in(key_of[6], 71), 0),
        "shifts": draw_shifts(jax.random.fold_in(key_of[6], 71), 0),
    }


DIFFUSION = 0.5
REACTION = 1.0


def legendre_pair(degree, point):
    previous_term, current_term = 1.0, point
    for degree_now in range(1, degree):
        previous_term, current_term = current_term, ((2 * degree_now + 1) * point * current_term - degree_now * previous_term) / (degree_now + 1)
    return current_term, previous_term


def radau_value(count, point):
    high_term, low_term = legendre_pair(count, point)
    return high_term - low_term


def radau_points(count):
    roots_found = []
    samples = 4000
    for sample_index in range(samples):
        left_end = -1.0 + 2.0 * sample_index / samples
        right_end = -1.0 + 2.0 * (sample_index + 1) / samples
        if radau_value(count, left_end) * radau_value(count, right_end) < 0.0:
            for halving in range(200):
                middle = 0.5 * (left_end + right_end)
                if radau_value(count, left_end) * radau_value(count, middle) <= 0.0:
                    right_end = middle
                else:
                    left_end = middle
            roots_found.append(0.5 * (left_end + right_end))
    roots_found.append(1.0)
    return [(root_value + 1.0) / 2.0 for root_value in roots_found]


def collocation_matrix(node_count):
    points = radau_points(node_count)
    node_table = [[0.0] * node_count for row_number in range(node_count)]
    for column in range(node_count):
        coeffs = [1.0]
        for another in range(node_count):
            if another != column:
                spacing = points[column] - points[another]
                raised = [0.0] + coeffs
                lowered = [entry * points[another] for entry in coeffs] + [0.0]
                coeffs = [(first_entry - second_entry) / spacing for first_entry, second_entry in zip(raised, lowered)]
        integral = [0.0] + [entry / (exponent_index + 1) for exponent_index, entry in enumerate(coeffs)]
        for row_number in range(node_count):
            running = 0.0
            for exponent_index in range(len(integral) - 1, -1, -1):
                running = running * points[row_number] + integral[exponent_index]
            node_table[row_number][column] = running
    return node_table


def fourier_tables(length):
    indices = jnp.arange(length, dtype=jnp.int32)
    product = (indices[:, None] * indices[None, :]) % length
    angles = product.astype(jnp.float32) * (2.0 * math.pi / length)
    return jnp.cos(angles), jnp.sin(angles)


def neighbours(padded):
    middle = padded[..., 1:-1, :, :]
    running = padded[..., 2:, :, :] + padded[..., :-2, :, :]
    widths = [(0, 0)] * (middle.ndim - 2) + [(1, 1), (0, 0)]
    across = jnp.pad(middle, widths)
    running = running + across[..., 2:, :] + across[..., :-2, :]
    widths = [(0, 0)] * (middle.ndim - 1) + [(1, 1)]
    across = jnp.pad(middle, widths)
    return running + across[..., 2:] + across[..., :-2]


def pad_depth(grid_field):
    widths = [(0, 0)] * (grid_field.ndim - 3) + [(1, 1), (0, 0), (0, 0)]
    return jnp.pad(grid_field, widths)


def shift_terms(shifts):
    shift_re = shifts[0][:, :, None, None, None]
    shift_im = shifts[1][:, :, None, None, None]
    coef_re = DIFFUSION * shift_re
    coef_im = DIFFUSION * shift_im
    diag_re = 1.0 + (6.0 * DIFFUSION - REACTION) * shift_re
    diag_im = (6.0 * DIFFUSION - REACTION) * shift_im
    magnitude = diag_re * diag_re + diag_im * diag_im
    return (coef_re, coef_im, diag_re / magnitude, -diag_im / magnitude)


def scale_rows(source, shift_coefs):
    inv_re, inv_im = shift_coefs[2], shift_coefs[3]
    return jnp.stack([source[0] * inv_re - source[1] * inv_im, source[0] * inv_im + source[1] * inv_re])


def sweep_rows(padded, source, shift_coefs):
    coef_re, coef_im, inv_re, inv_im = shift_coefs
    beside_all = neighbours(padded)
    target_re = source[0] + coef_re * beside_all[0] - coef_im * beside_all[1]
    target_im = source[1] + coef_re * beside_all[1] + coef_im * beside_all[0]
    return jnp.stack([target_re * inv_re - target_im * inv_im, target_re * inv_im + target_im * inv_re])


def reaction_residual(grid_field, initial_value, node_rows):
    forcing = DIFFUSION * (neighbours(pad_depth(grid_field)) - 6.0 * grid_field) + REACTION * (grid_field - grid_field * grid_field * grid_field)
    mixed_terms = jnp.einsum("mj,sjzxy->smzxy", node_rows, forcing, precision=lax.Precision.HIGHEST)
    final_node = grid_field[:, -1]
    previous = jnp.concatenate([initial_value[None], final_node[:-1]], 0)
    return previous[:, None] + mixed_terms - grid_field


def complex_mix(matrix_pair, real_part, imag_part, form):
    high = lax.Precision.HIGHEST
    out_re = jnp.einsum(form, matrix_pair[0], real_part, precision=high) - jnp.einsum(form, matrix_pair[1], imag_part, precision=high)
    out_im = jnp.einsum(form, matrix_pair[0], imag_part, precision=high) + jnp.einsum(form, matrix_pair[1], real_part, precision=high)
    return out_re, out_im


def reference(iterate, initial_value, alpha_power, node_mix, node_back, shifts):
    high = lax.Precision.HIGHEST
    node_rows = jnp.asarray(collocation_matrix(NODES), jnp.float32)
    residual = reaction_residual(iterate, initial_value, node_rows)
    exponent = alpha_power[0].astype(jnp.float32) / 16.0
    step_values = jnp.arange(STEPS, dtype=jnp.int32).astype(jnp.float32)
    step_scale = jnp.exp2(-exponent * step_values / STEPS)[:, None, None, None, None]
    scaled = residual * step_scale
    cosine, sine_table = fourier_tables(STEPS)
    spec_re = jnp.einsum("kn,nmzxy->kmzxy", cosine, scaled, precision=high)
    spec_im = -jnp.einsum("kn,nmzxy->kmzxy", sine_table, scaled, precision=high)
    source_re, source_im = complex_mix(node_mix, spec_re, spec_im, "kmj,kjzxy->kmzxy")
    source = jnp.stack([source_re, source_im])
    shift_coefs = shift_terms(shifts)
    solved = scale_rows(source, shift_coefs)
    for sweep_index in range(SWEEPS - 1):
        solved = sweep_rows(pad_depth(solved), source, shift_coefs)
    backed_re, backed_im = complex_mix(node_back, solved[0], solved[1], "kmj,kjzxy->kmzxy")
    correction = jnp.einsum("nk,kmzxy->nmzxy", cosine, backed_re, precision=high) - jnp.einsum("nk,kmzxy->nmzxy", sine_table, backed_im, precision=high)
    back_scale = (jnp.exp2(exponent * step_values / STEPS) / STEPS)[:, None, None, None, None]
    updated = iterate + correction * back_scale
    return updated, reaction_residual(updated, initial_value, node_rows)
```

```python
import math

import jax
import jax.numpy as jnp
import numpy as np
from jax import lax
from jax.sharding import PartitionSpec as P

STEPS = 16
NODES = 4
SWEEPS = 8
GX = 32
GY = 256
NZ = 64

DIFFUSION = 0.5
REACTION = 1.0
HIGH = lax.Precision.HIGHEST


def legendre_pair(degree, point):
    previous_term, current_term = (1.0, point)
    for degree_now in range(1, degree):
        previous_term, current_term = (
            current_term,
            ((2 * degree_now + 1) * point * current_term - degree_now * previous_term)
            / (degree_now + 1),
        )
    return (current_term, previous_term)


def radau_value(count, point):
    high_term, low_term = legendre_pair(count, point)
    return high_term - low_term


def radau_points(count):
    roots_found = []
    samples = 4000
    for sample_index in range(samples):
        left_end = -1.0 + 2.0 * sample_index / samples
        right_end = -1.0 + 2.0 * (sample_index + 1) / samples
        if radau_value(count, left_end) * radau_value(count, right_end) < 0.0:
            for halving in range(200):
                middle = 0.5 * (left_end + right_end)
                if radau_value(count, left_end) * radau_value(count, middle) <= 0.0:
                    right_end = middle
                else:
                    left_end = middle
            roots_found.append(0.5 * (left_end + right_end))
    roots_found.append(1.0)
    return [(root_value + 1.0) / 2.0 for root_value in roots_found]


def collocation_matrix(node_count):
    points = radau_points(node_count)
    node_table = [[0.0] * node_count for row_number in range(node_count)]
    for column in range(node_count):
        coeffs = [1.0]
        for another in range(node_count):
            if another != column:
                spacing = points[column] - points[another]
                raised = [0.0] + coeffs
                lowered = [entry * points[another] for entry in coeffs] + [0.0]
                coeffs = [
                    (first_entry - second_entry) / spacing
                    for first_entry, second_entry in zip(raised, lowered)
                ]
        integral = [0.0] + [
            entry / (exponent_index + 1) for exponent_index, entry in enumerate(coeffs)
        ]
        for row_number in range(node_count):
            running = 0.0
            for exponent_index in range(len(integral) - 1, -1, -1):
                running = running * points[row_number] + integral[exponent_index]
            node_table[row_number][column] = running
    return node_table


def sine_matrix(count):
    index = np.arange(1, count + 1)
    return math.sqrt(2.0 / (count + 1)) * np.sin(np.pi * np.outer(index, index) / (count + 1))


def eigenvalues(count):
    return 2.0 * np.cos(np.pi * np.arange(1, count + 1) / (count + 1))


def tables():
    coll = np.array(collocation_matrix(NODES))
    sx, sy, sz = (sine_matrix(n) for n in (GX, GY, NZ))
    kx = np.einsum("kx,fg->kfgx", sx, np.eye(8)).reshape(256, 256)
    n = np.arange(STEPS)
    real_dft = np.zeros((8, 2, STEPS))
    for q in range(8):
        real_dft[q, 0] = np.cos(2 * np.pi * q * n / STEPS)
        real_dft[q, 1] = -np.sin(2 * np.pi * q * n / STEPS) if q else np.cos(np.pi * n)
    shifted = np.zeros_like(real_dft)
    shifted[:, :, :-1] = real_dft[:, :, 1:]
    split = real_dft.reshape(8, 2, 8, 2)
    shifted = shifted.reshape(8, 2, 8, 2)
    nodes = np.eye(NODES).reshape(NODES, 2, 2)
    last = np.zeros((NODES, 2, 2))
    last[:, 1, 1] = 1.0
    two = np.eye(2)
    form = "qrsn,mtj,kl,zw->qkrmzstlnjw"
    mu0 = -np.einsum(form, split, nodes, two, two).reshape(256, 256)
    mu1 = np.einsum(form, shifted, last, two, two).reshape(256, 256)
    mf = np.einsum(form, split, coll.reshape(NODES, 2, 2), two, two).reshape(256, 256)
    mi = np.einsum("qrsn,mtj,kl,zw->stlnjwqkrmz", split, nodes, two, two).reshape(256, 256)
    zf = np.einsum("rp,mn,ksz->rmkspnz", two, np.eye(4), sz.reshape(NZ, 32, 2)).reshape(512, 512)
    lam_z, lam_x, lam_y = (eigenvalues(n) for n in (NZ, GX, GY))
    start = np.linalg.solve(coll, np.ones(NODES))
    return dict(coll=coll, sy=sy, kx=kx, mu0=mu0, mu1=mu1, mf=mf, mi=mi, zf=zf, lam_z=lam_z,
                lam_x=lam_x, lam_y=lam_y, start=start)


TABLES = tables()


def table(name):
    return jnp.asarray(TABLES[name], jnp.float32)


def dot(a, b):
    return jnp.dot(a, b, precision=HIGH, preferred_element_type=jnp.float32)


def in_plane(v):
    out = jnp.zeros_like(v)
    pad = [(0, 0)] * (v.ndim - 2)
    a = jnp.pad(v, pad + [(1, 1), (0, 0)])
    b = jnp.pad(v, pad + [(0, 0), (1, 1)])
    return a[..., 2:, :] + a[..., :-2, :] + b[..., 2:] + b[..., :-2]


def on_device(iterate, initial_value, alpha_power, node_mix, node_back, shifts):
    step, node, space = (lax.axis_index(a) for a in ("step", "node", "space"))
    ring_up = [(i, (i + 1)) for i in range(31)]
    ring_down = [(i + 1, i) for i in range(31)]
    below = lax.ppermute(iterate[:, :, 1:], "space", ring_up)
    above = lax.ppermute(iterate[:, :, :1], "space", ring_down)
    padded = jnp.concatenate([below, iterate, above], 2)
    nb = padded[:, :, 2:] + padded[:, :, :-2] + in_plane(iterate)
    forcing = DIFFUSION * (nb - 6.0 * iterate) + REACTION * (iterate - iterate * iterate * iterate)
    start = lax.dynamic_slice_in_dim(table("start"), node * 2, 2)
    first = jnp.where(step == 0, start, 0.0)[:, None, None, None] * initial_value[None]
    forcing = jnp.concatenate([forcing[:1] + first[None], forcing[1:]], 0)

    sy, kx = table("sy"), table("kx")
    uh = dot(kx, dot(iterate.reshape(256, 256), sy))
    fh = dot(kx, dot(forcing.reshape(256, 256), sy))
    sent = jnp.stack([uh.reshape(16, 16, 256), fh.reshape(16, 16, 256)], 1)
    got = lax.all_to_all(sent, ("step", "node"), 0, 0, tiled=True)
    ru, rf = got[:, 0].reshape(256, 256), got[:, 1].reshape(256, 256)

    exponent = alpha_power[0].astype(jnp.float32) / 16.0 / STEPS
    n_of = (np.arange(256) // 32) * 2 + (np.arange(256) // 4) % 2
    n_of = jnp.asarray(n_of, jnp.float32)
    scale0 = jnp.exp2(-exponent * n_of)
    scale1 = jnp.exp2(-exponent * (n_of + 1.0))
    mu = table("mu0") * scale0[None] + table("mu1") * scale1[None]
    mf = table("mf") * scale0[None]
    spec = dot(mu, ru) + dot(mf, rf)

    spec = spec.reshape(16, 16, 2, 128).transpose(0, 2, 1, 3).reshape(32, 16, 128)
    spec = lax.all_to_all(spec, "space", 0, 0, tiled=True).reshape(512, 128)
    s = dot(table("zf"), spec).reshape(2, 4, 64, 128)

    q = space // 4
    kk = (space // 2) % 2
    h = space % 2
    p = step * 2 + node
    params = [lax.all_gather(lax.all_gather(x, "step", axis=1, tiled=True), "node", axis=2, tiled=True)
              for x in (node_mix, node_back, shifts)]
    def of(x, k):
        return lax.complex(*[lax.dynamic_index_in_dim(x[c], k, 0, keepdims=False) for c in (0, 1)])
    def coefs(k):
        d = of(params[2], k)
        b = 1.0 + 2.0 * d
        r = 0.5 * d / b
        g = jnp.stack([r ** j / b for j in range(SWEEPS)])
        return jnp.sum(of(params[1], k)[None, :, :, None] * g[:, None, :, None] * of(params[0], k)[None, None], 2)
    ck, cp = coefs(q), coefs(jnp.where(q == 0, 8, 16 - q))
    ca = jnp.where(q == 0, ck.real, ck.real + cp.real)
    ce = jnp.where(q == 0, 0.0, ck.imag - cp.imag)
    cd = jnp.where(q == 0, cp.real, ck.real + cp.real)
    lam_x = lax.dynamic_index_in_dim(table("lam_x"), 2 * p + kk, 0, keepdims=False)
    lam_y = lax.dynamic_slice_in_dim(table("lam_y"), h * 128, 128)
    lam = table("lam_z")[:, None] + lam_y[None] + lam_x
    def horner(c):
        acc = c[-1]
        for j in range(SWEEPS - 2, -1, -1):
            acc = acc * lam + c[j]
        return acc
    def apply(c, v):
        return jnp.stack([sum(horner(c[:, i, j]) * v[j] for j in range(4)) for i in range(4)])
    out = jnp.stack([apply(ca, s[0]) - apply(ce, s[1]), apply(ce, s[0]) + apply(cd, s[1])])

    back = dot(table("zf").T, out.reshape(512, 128)).reshape(32, 16, 128)
    back = lax.all_to_all(back, "space", 0, 0, tiled=True)
    back = back.reshape(16, 2, 16, 128).transpose(0, 2, 1, 3).reshape(256, 256)
    mi = table("mi") * (jnp.exp2(exponent * n_back()) / STEPS)[:, None]
    corr = dot(mi, back).reshape(8, 1, 2, 16, 256)
    corr = jnp.broadcast_to(corr, (8, 2, 2, 16, 256)).reshape(16, 2, 16, 256)
    corr = lax.all_to_all(corr, ("step", "node"), 0, 0, tiled=True)
    corr = corr.transpose(1, 0, 2, 3).reshape(2, 256, 256)
    corr = jnp.stack([dot(dot(kx.T, corr[g]), sy) for g in range(2)]).reshape(2, 2, 2, 2, 32, 256)

    other = lax.ppermute(iterate, "node", [(0, 1), (1, 0)])
    both = jnp.where(node == 0, jnp.stack([iterate, other]), jnp.stack([other, iterate]))
    both = both + corr
    updated = lax.dynamic_index_in_dim(both, node, 0, keepdims=False)
    u = both.transpose(1, 0, 2, 3, 4, 5).reshape(2, 4, 2, 32, 256)
    rows = lax.dynamic_slice_in_dim(table("coll"), node * 2, 2, 0)
    mixed = DIFFUSION * (in_plane(u) + u[:, :, ::-1]) + (REACTION - 6.0 * DIFFUSION) * u - REACTION * u * u * u
    mixed = jnp.einsum("mj,njzxy->nmzxy", rows, mixed, precision=HIGH)
    edge = DIFFUSION * jnp.einsum("mj,njzxy->nmzxy", rows, u, precision=HIGH)
    below = lax.ppermute(edge[:, :, 1:], "space", ring_up)
    above = lax.ppermute(edge[:, :, :1], "space", ring_down)
    mixed = mixed + jnp.concatenate([below, above], 2)
    before = lax.ppermute(u[1, 3], "step", [(i, i + 1) for i in range(7)])
    before = jnp.where(step == 0, initial_value, before)
    previous = jnp.stack([before, u[0, 3]])
    return updated, previous[:, None] + mixed - updated


def n_back():
    return jnp.asarray((np.arange(256) // 32) * 2 + (np.arange(256) // 4) % 2, jnp.float32)


def solution(mesh):
    in_specs = (
        P("step", "node", "space", None, None),
        P("space", None, None),
        P(),
        P(None, "step", "node", None),
        P(None, "step", "node", None),
        P(None, "step", "node"),
    )
    out_specs = (P("step", "node", "space", None, None), P("step", "node", "space", None, None))
    return jax.shard_map(
        on_device, mesh=mesh, in_specs=in_specs, out_specs=out_specs, check_vma=False
    )
```

```python
import math

import jax
import jax.numpy as jnp
import numpy as np
from jax import lax
from jax.experimental import pallas as pl
from jax.experimental.pallas import tpu as pltpu
from jax.sharding import PartitionSpec as P

STEPS = 16
NODES = 4
SWEEPS = 8
GX = 32
GY = 256
NZ = 64

DIFFUSION = 0.5
REACTION = 1.0
HIGH = lax.Precision.HIGHEST


def legendre_pair(degree, point):
    previous_term, current_term = (1.0, point)
    for degree_now in range(1, degree):
        previous_term, current_term = (
            current_term,
            ((2 * degree_now + 1) * point * current_term - degree_now * previous_term)
            / (degree_now + 1),
        )
    return (current_term, previous_term)


def radau_value(count, point):
    high_term, low_term = legendre_pair(count, point)
    return high_term - low_term


def radau_points(count):
    roots_found = []
    samples = 4000
    for sample_index in range(samples):
        left_end = -1.0 + 2.0 * sample_index / samples
        right_end = -1.0 + 2.0 * (sample_index + 1) / samples
        if radau_value(count, left_end) * radau_value(count, right_end) < 0.0:
            for halving in range(200):
                middle = 0.5 * (left_end + right_end)
                if radau_value(count, left_end) * radau_value(count, middle) <= 0.0:
                    right_end = middle
                else:
                    left_end = middle
            roots_found.append(0.5 * (left_end + right_end))
    roots_found.append(1.0)
    return [(root_value + 1.0) / 2.0 for root_value in roots_found]


def collocation_matrix(node_count):
    points = radau_points(node_count)
    node_table = [[0.0] * node_count for row_number in range(node_count)]
    for column in range(node_count):
        coeffs = [1.0]
        for another in range(node_count):
            if another != column:
                spacing = points[column] - points[another]
                raised = [0.0] + coeffs
                lowered = [entry * points[another] for entry in coeffs] + [0.0]
                coeffs = [
                    (first_entry - second_entry) / spacing
                    for first_entry, second_entry in zip(raised, lowered)
                ]
        integral = [0.0] + [
            entry / (exponent_index + 1) for exponent_index, entry in enumerate(coeffs)
        ]
        for row_number in range(node_count):
            running = 0.0
            for exponent_index in range(len(integral) - 1, -1, -1):
                running = running * points[row_number] + integral[exponent_index]
            node_table[row_number][column] = running
    return node_table


def sine_matrix(count):
    index = np.arange(1, count + 1)
    return math.sqrt(2.0 / (count + 1)) * np.sin(np.pi * np.outer(index, index) / (count + 1))


def eigenvalues(count):
    return 2.0 * np.cos(np.pi * np.arange(1, count + 1) / (count + 1))


def tables():
    coll = np.array(collocation_matrix(NODES))
    sx, sy, sz = (sine_matrix(n) for n in (GX, GY, NZ))
    kx = np.einsum("kx,fg->kfgx", sx, np.eye(8)).reshape(256, 256)
    n = np.arange(STEPS)
    real_dft = np.zeros((8, 2, STEPS))
    for q in range(8):
        real_dft[q, 0] = np.cos(2 * np.pi * q * n / STEPS)
        real_dft[q, 1] = -np.sin(2 * np.pi * q * n / STEPS) if q else np.cos(np.pi * n)
    shifted = np.zeros_like(real_dft)
    shifted[:, :, :-1] = real_dft[:, :, 1:]
    split = real_dft.reshape(8, 2, 8, 2)
    shifted = shifted.reshape(8, 2, 8, 2)
    nodes = np.eye(NODES).reshape(NODES, 2, 2)
    last = np.zeros((NODES, 2, 2))
    last[:, 1, 1] = 1.0
    two = np.eye(2)
    form = "qrsn,mtj,kl,zw->qkrmzstlnjw"
    mu0 = -np.einsum(form, split, nodes, two, two).reshape(256, 256)
    mu1 = np.einsum(form, shifted, last, two, two).reshape(256, 256)
    mf = np.einsum(form, split, coll.reshape(NODES, 2, 2), two, two).reshape(256, 256)
    mi = np.einsum("qrsn,mtj,kl,zw->stlnjwqkrmz", split, nodes, two, two).reshape(256, 256)
    zf = np.einsum("rp,mn,ksz->rmkspnz", two, np.eye(4), sz.reshape(NZ, 32, 2)).reshape(512, 512)
    lam_z, lam_x, lam_y = (eigenvalues(n) for n in (NZ, GX, GY))
    lam_xy = np.repeat(lam_x, 8)[:, None] + lam_y[None]
    lam_zy = lam_z[None, :, None] + lam_y.reshape(2, 1, 128)
    lam_x = np.broadcast_to(lam_x[:, None, None], (GX, 8, 128))
    start = np.linalg.solve(coll, np.ones(NODES))
    arrays = dict(sy=sy, kx=kx, lam_xy=lam_xy, mu0=mu0, mu1=mu1, mf=mf, zf=zf, zt=zf.T, mi=mi,
                  kt=kx.T, lam_zy=lam_zy, lam_x=lam_x)
    return coll, start, {k: np.asarray(v, np.float32) for k, v in arrays.items()}


COLL, START, TABLES = tables()
NAMES = tuple(TABLES)


def dot(a, b):
    return jnp.dot(a, b, precision=HIGH, preferred_element_type=jnp.float32)


def horner_tables(q, params, coef, tab, lam):
    partner = (16 - q) % 16 + 8 * ((8 - q) // 8)
    own = params[2 * (q // 2)] + params[2 * (q // 2) + 1]
    mate = params[2 * (partner // 2)] + params[2 * (partner // 2) + 1]
    row = lax.broadcasted_iota(jnp.int32, (8, 128), 0)
    odd = q % 2 == 1
    own = jnp.where(odd, pltpu.roll(own, 4, 0), own)
    mate = jnp.where(odd, mate, pltpu.roll(mate, 4, 0))
    x = jnp.where(row < 4, own, mate)
    bre, bim, mre, mim, dre, dim = [x if c == 0 else pltpu.roll(x, 128 - 16 * c, 1) for c in range(6)]
    pre, pim = bre * mre - bim * mim, bre * mim + bim * mre
    scale = 6.0 * DIFFUSION - REACTION
    ere, eim = 1.0 + scale * dre, scale * dim
    mag = ere * ere + eim * eim
    gre, gim = ere / mag, -eim / mag
    are, aim = DIFFUSION * dre, DIFFUSION * dim
    rre, rim = are * gre - aim * gim, are * gim + aim * gre
    first = q == 0
    for power in range(SWEEPS):
        tre, tim = pre * gre - pim * gim, pre * gim + pim * gre
        gre, gim = gre * rre - gim * rim, gre * rim + gim * rre
        kre, kim = (jnp.sum(v[0:4], axis=0, keepdims=True) for v in (tre, tim))
        ore, oim = (jnp.sum(v[4:8], axis=0, keepdims=True) for v in (tre, tim))
        both = kre + ore
        coef[0, power : power + 1, :] = jnp.where(first, kre, both)
        coef[1, power : power + 1, :] = jnp.where(first, 0.0, kim - oim)
        coef[2, power : power + 1, :] = jnp.where(first, ore, both)

    def entry(e, carry):
        following = []
        for a, c in enumerate(carry):
            col = jnp.broadcast_to(c[:, 0:1], (8, 128))
            acc = jnp.broadcast_to(col[SWEEPS - 1 : SWEEPS], (64, 128))
            for power in range(SWEEPS - 2, -1, -1):
                acc = acc * lam + col[power : power + 1]
            tab[a, e] = acc
            following.append(pltpu.roll(c, 127, 1))
        return tuple(following)

    lax.fori_loop(0, 16, entry, (coef[0], coef[1], coef[2]))


def pack_params(node, mix, back, shifts, out):
    row = lax.broadcasted_iota(jnp.int32, (8, 128), 0)
    lane = lax.broadcasted_iota(jnp.int32, (8, 128), 1)
    kind, i, j = lane // 16, (lane // 4) % 4, lane % 4
    k, m = row // 4, row % 4
    acc = jnp.zeros((8, 128), jnp.float32)
    for c in range(2):
        for kk in range(2):
            here = k == kk
            for l in range(2):
                mine = 2 * node + l
                at_mix = here & (kind == 2 + c) & (m == mine)
                at_back = here & (kind == c) & (i == mine)
                for n in range(4):
                    acc = jnp.where(at_mix & (j == n), mix[c, kk, l, n], acc)
                    acc = jnp.where(at_back & (m == n), back[c, kk, l, n], acc)
                acc = jnp.where(here & (kind == 4 + c) & (m == mine), shifts[c, kk, l], acc)
    out[...] = acc


def kernel(u_ref, init_ref, alpha_ref, mix_ref, back_ref, shifts_ref, *refs):
    consts = dict(zip(NAMES, refs[: len(NAMES)]))
    refs = refs[len(NAMES) :]
    out_u, out_r = refs[:2]
    refs = refs[2:]
    held = dict(zip(NAMES, refs[: len(NAMES)]))
    refs = refs[len(NAMES) :]
    (su, ru, sf, rf, sp, rp, s2, r2, s3, r3, s4, r4, halo, grid, ub, wb, whalo, before, coef, tab,
     sw, ow, load_sem, send_sem, recv_sem) = refs
    step, node, space = (lax.axis_index(a) for a in ("step", "node", "space"))
    me = step * 2 + node

    loads = {}
    for index, name in enumerate(NAMES):
        loads[name] = pltpu.make_async_copy(consts[name], held[name], load_sem.at[index])
        loads[name].start()

    def get(name):
        loads[name].wait()
        return held[name]

    barrier = pltpu.get_barrier_semaphore()

    def group_id(d):
        other = (me + d) % 16
        return other, {"step": other // 2, "node": other % 2}

    def greet_group(d, _):
        pl.semaphore_signal(barrier, inc=1, device_id=group_id(d)[1])
        return 0

    def greet_space(d, _):
        pl.semaphore_signal(barrier, inc=1, device_id={"space": (space + d) % 32})
        return 0

    lax.fori_loop(1, 16, greet_group, 0)
    lax.fori_loop(1, 32, greet_space, 0)
    pl.semaphore_wait(barrier, 46)

    def remote(src, dst, sem, device):
        return pltpu.make_async_remote_copy(
            src_ref=src, dst_ref=dst, send_sem=send_sem.at[sem], recv_sem=recv_sem.at[sem], device_id=device
        )

    up, down = {"space": (space + 1) % 32}, {"space": (space + 31) % 32}
    HALO_UP, HALO_DOWN, GROUP_U, GROUP_F, PARAMS, SPACE, BACK, CORR, OTHER, W_UP, W_DOWN, BEFORE = range(12)
    pending = [
        remote(u_ref.at[:, 1], halo.at[0], HALO_UP, up),
        remote(u_ref.at[:, 0], halo.at[1], HALO_DOWN, down),
    ]
    for copy in pending:
        copy.start()

    def to_group(src, dst, sem):
        def body(d, _):
            other, device = group_id(d)
            remote(src.at[other], dst.at[me], sem, device).start()
            return 0
        lax.fori_loop(1, 16, body, 0)
        dst[me] = src[me]

    def to_space(src, dst, sem):
        def body(d, _):
            other = (space + d) % 32
            remote(src.at[other], dst.at[space], sem, {"space": other}).start()
            return 0
        lax.fori_loop(1, 32, body, 0)
        dst[space] = src[space]

    def arrived(ref, sem, count):
        part = ref.at[pl.ds(0, count)]
        remote(part, part, sem, up).wait_recv()

    def sent(ref, sem, count):
        part = ref.at[pl.ds(0, count)]
        remote(part, part, sem, up).wait_send()

    sy, kx = get("sy"), get("kx")
    uh = dot(kx[...], dot(u_ref[...].reshape(256, 256), sy[...]))
    su[...] = uh.reshape(16, 16, 256)
    to_group(su, ru, GROUP_U)

    low = jnp.where(space == 0, 0.0, DIFFUSION)
    high = jnp.where(space == 31, 0.0, DIFFUSION)
    begin = [
        jnp.where(step == 0, jnp.where(node == 0, START[m], START[2 + m]), 0.0).astype(jnp.float32) for m in range(2)
    ]
    pending[0].wait_recv()
    pending[1].wait_recv()
    for nm in range(4):
        for z in range(2):
            u = u_ref[nm, z]
            beside = DIFFUSION * u_ref[nm, 1 - z] + (low if z == 0 else high) * halo[z, nm]
            value = beside - (6.0 * DIFFUSION - REACTION) * u - REACTION * (u * u * u)
            if nm < 2:
                value = value + begin[nm] * init_ref[z]
            grid[nm * 2 + z] = value
    fh = dot(kx[...], dot(grid[...].reshape(256, 256), sy[...]))
    fh = fh + DIFFUSION * get("lam_xy")[...] * su[...].reshape(256, 256)
    sf[...] = fh.reshape(16, 16, 256)
    to_group(sf, rf, GROUP_F)

    pack_params(node, mix_ref, back_ref, shifts_ref, sp)

    def send_params(d, _):
        remote(sp, rp.at[me], PARAMS, group_id(d)[1]).start()
        return 0

    lax.fori_loop(1, 16, send_params, 0)
    rp[me] = sp[...]

    rate = alpha_ref[0].astype(jnp.float32) * (math.log(2.0) / 16.0 / STEPS)
    col = lax.broadcasted_iota(jnp.int32, (1, 256), 1)
    when = (2 * (col // 32) + (col // 4) % 2).astype(jnp.float32)
    scale0, scale1 = jnp.exp(-rate * when), jnp.exp(-rate * (when + 1.0))
    mu = get("mu0")[...] * scale0 + get("mu1")[...] * scale1
    mf = get("mf")[...] * scale0
    arrived(ru, GROUP_U, 15)
    spec = dot(mu, ru[...].reshape(256, 256))
    arrived(rf, GROUP_F, 15)
    spec = spec + dot(mf, rf[...].reshape(256, 256))
    for h in range(2):
        s2[:, h] = spec[:, h * 128 : h * 128 + 128].reshape(16, 16, 128)
    s2_flat, r2_flat = s2.reshape(32, 16, 128), r2
    to_space(s2_flat, r2_flat, SPACE)
    other_u = remote(u_ref, ub.at[node], OTHER, {"node": 1 - node})
    other_u.start()
    ub[node] = u_ref[...]

    arrived(rp, PARAMS, 15)
    q = space // 4
    lam = get("lam_zy")[space % 2] + jnp.broadcast_to(
        get("lam_x")[2 * me + (space // 2) % 2][0:1], (64, 128))
    horner_tables(q, rp, coef, tab, lam)
    row = lax.broadcasted_iota(jnp.int32, (256, 256), 0)
    when = (2 * (row // 32) + (row // 4) % 2).astype(jnp.float32)
    held["mi"][...] = get("mi")[...] * (jnp.exp(rate * when) * (1.0 / STEPS))

    zf, zt = get("zf"), get("zt")
    arrived(r2_flat, SPACE, 31)
    sw[...] = dot(zf[...], r2[...].reshape(512, 128)).reshape(8, 64, 128)

    def solve(z, _):
        at = pl.ds(pl.multiple_of(z * 8, 8), 8)
        s = [sw[i, at, :] for i in range(8)]
        for i in range(4):
            re = im = None
            for j in range(4):
                a, e, d = (tab[c, 4 * i + j, at, :] for c in range(3))
                tre, tim = a * s[j] - e * s[4 + j], e * s[j] + d * s[4 + j]
                re, im = (tre, tim) if re is None else (re + tre, im + tim)
            ow[i, at, :] = re
            ow[4 + i, at, :] = im
        return 0

    lax.fori_loop(0, 8, solve, 0)
    s3[...] = dot(zt[...], ow[...].reshape(512, 128)).reshape(32, 16, 128)
    to_space(s3, r3, BACK)
    kt = get("kt")
    arrived(r3, BACK, 31)
    for h in range(2):
        part = r3[...].reshape(16, 2, 16, 128)[:, h].reshape(256, 128)
        s4[:, :, :, h * 128 : h * 128 + 128] = dot(held["mi"][...], part).reshape(8, 2, 16, 128)

    def send_corr(d, _):
        other, device = group_id(d)
        remote(s4.at[other // 2], r4.at[:, me], CORR, device).start()
        return 0

    lax.fori_loop(1, 16, send_corr, 0)
    r4[:, me] = s4[step]
    other_u.wait_recv()
    whole = r4.at[:, pl.ds(0, 15)]
    remote(whole, whole, CORR, up).wait_recv()
    for g in range(2):
        d = dot(dot(kt[...], r4[g].reshape(256, 256)), sy[...])
        ub[g] = ub[g] + d.reshape(4, 2, 32, 256)
    out_u[...] = ub[node]

    weight = [
        [jnp.where(node == 0, COLL[m][j], COLL[2 + m][j]).astype(jnp.float32) for j in range(4)] for m in range(2)
    ]

    def nodes_at(n, z):
        return [ub[j // 2, 2 * n + j % 2, z] for j in range(4)]

    for n in range(2):
        for z in range(2):
            u = nodes_at(n, z)
            for m in range(2):
                wb[2 * n + m, z] = sum(weight[m][j] * u[j] for j in range(4))
    last = [
        remote(wb.at[:, 1], whalo.at[0], W_UP, up),
        remote(wb.at[:, 0], whalo.at[1], W_DOWN, down),
        remote(ub.at[1, 3], before, BEFORE, {"step": (step + 1) % 8}),
    ]
    for copy in last:
        copy.start()
    x = lax.broadcasted_iota(jnp.int32, (32, 256), 0)
    y = lax.broadcasted_iota(jnp.int32, (32, 256), 1)
    for n in range(2):
        for z in range(2):
            cubes = [v * v * v for v in nodes_at(n, z)]
            for m in range(2):
                w = wb[2 * n + m, z]
                beside = (
                    wb[2 * n + m, 1 - z]
                    + jnp.where(x == 0, 0.0, pltpu.roll(w, 1, 0))
                    + jnp.where(x == 31, 0.0, pltpu.roll(w, 31, 0))
                    + jnp.where(y == 0, 0.0, pltpu.roll(w, 1, 1))
                    + jnp.where(y == 255, 0.0, pltpu.roll(w, 255, 1))
                )
                value = DIFFUSION * beside - (6.0 * DIFFUSION - REACTION) * w
                value = value - REACTION * sum(weight[m][j] * cubes[j] for j in range(4)) - ub[node, 2 * n + m, z]
                if n == 1:
                    value = value + ub[1, 1, z]
                out_r[2 * n + m, z] = value
    for copy in last:
        copy.wait_recv()
    for z in range(2):
        opening = jnp.where(step == 0, init_ref[z], before[z])
        for nm in range(4):
            edge = (low if z == 0 else high) * whalo[z, nm]
            out_r[nm, z] = out_r[nm, z] + (edge + opening if nm < 2 else edge)

    for copy in pending + last + [other_u]:
        copy.wait_send()
    sent(su, GROUP_U, 15)
    sent(sf, GROUP_F, 15)
    sent(rp, PARAMS, 15)
    sent(s3, SPACE, 31)
    sent(s3, BACK, 31)
    remote(whole, whole, CORR, up).wait_send()


def on_device(iterate, initial_value, alpha_power, node_mix, node_back, shifts):
    consts = [jnp.asarray(TABLES[name]) for name in NAMES]
    f32 = jnp.float32
    vmem = lambda *shape: pltpu.VMEM(shape, f32)
    block = jax.ShapeDtypeStruct((4, 2, 32, 256), f32)
    in_vmem, in_smem = (pl.BlockSpec(memory_space=m) for m in (pltpu.VMEM, pltpu.SMEM))
    updated, residual = pl.pallas_call(
        kernel,
        out_shape=(block, block),
        in_specs=[in_vmem, in_vmem] + [in_smem] * 4 + [pl.BlockSpec(memory_space=pl.ANY)] * len(NAMES),
        out_specs=(in_vmem, in_vmem),
        scratch_shapes=[vmem(*TABLES[name].shape) for name in NAMES]
        + [vmem(16, 16, 256)] * 4
        + [vmem(8, 128), vmem(16, 8, 128)]
        + [vmem(16, 2, 16, 128), vmem(32, 16, 128)]
        + [vmem(32, 16, 128)] * 2
        + [vmem(8, 2, 16, 256), vmem(2, 16, 16, 256)]
        + [vmem(2, 4, 32, 256), vmem(8, 32, 256)]
        + [vmem(2, 4, 2, 32, 256), vmem(4, 2, 32, 256), vmem(2, 4, 32, 256), vmem(2, 32, 256)]
        + [vmem(3, 8, 128), vmem(3, 16, 64, 128)]
        + [vmem(8, 64, 128)] * 2
        + [pltpu.SemaphoreType.DMA((len(NAMES),)), pltpu.SemaphoreType.DMA((12,)), pltpu.SemaphoreType.DMA((12,))],
        compiler_params=pltpu.CompilerParams(
            collective_id=0, has_side_effects=True, vmem_limit_bytes=48 * 1024 * 1024
        ),
    )(iterate.reshape(4, 2, 32, 256), initial_value, alpha_power, node_mix, node_back, shifts, *consts)
    return updated.reshape(iterate.shape), residual.reshape(iterate.shape)


def solution(mesh):
    in_specs = (
        P("step", "node", "space", None, None),
        P("space", None, None),
        P(),
        P(None, "step", "node", None),
        P(None, "step", "node", None),
        P(None, "step", "node"),
    )
    out_specs = (P("step", "node", "space", None, None), P("step", "node", "space", None, None))
    return jax.shard_map(
        on_device, mesh=mesh, in_specs=in_specs, out_specs=out_specs, check_vma=False
    )
```

```python
import math

import jax
import jax.numpy as jnp
import numpy as np
from jax import lax
from jax.experimental import pallas as pl
from jax.experimental.pallas import tpu as pltpu
from jax.sharding import PartitionSpec as P

STEPS = 16
NODES = 4
SWEEPS = 8
GX = 32
GY = 256
NZ = 64

DIFFUSION = 0.5
REACTION = 1.0
HIGH = lax.Precision.HIGHEST


def legendre_pair(degree, point):
    previous_term, current_term = (1.0, point)
    for degree_now in range(1, degree):
        previous_term, current_term = (
            current_term,
            ((2 * degree_now + 1) * point * current_term - degree_now * previous_term)
            / (degree_now + 1),
        )
    return (current_term, previous_term)


def radau_value(count, point):
    high_term, low_term = legendre_pair(count, point)
    return high_term - low_term


def radau_points(count):
    roots_found = []
    samples = 4000
    for sample_index in range(samples):
        left_end = -1.0 + 2.0 * sample_index / samples
        right_end = -1.0 + 2.0 * (sample_index + 1) / samples
        if radau_value(count, left_end) * radau_value(count, right_end) < 0.0:
            for halving in range(200):
                middle = 0.5 * (left_end + right_end)
                if radau_value(count, left_end) * radau_value(count, middle) <= 0.0:
                    right_end = middle
                else:
                    left_end = middle
            roots_found.append(0.5 * (left_end + right_end))
    roots_found.append(1.0)
    return [(root_value + 1.0) / 2.0 for root_value in roots_found]


def collocation_matrix(node_count):
    points = radau_points(node_count)
    node_table = [[0.0] * node_count for row_number in range(node_count)]
    for column in range(node_count):
        coeffs = [1.0]
        for another in range(node_count):
            if another != column:
                spacing = points[column] - points[another]
                raised = [0.0] + coeffs
                lowered = [entry * points[another] for entry in coeffs] + [0.0]
                coeffs = [
                    (first_entry - second_entry) / spacing
                    for first_entry, second_entry in zip(raised, lowered)
                ]
        integral = [0.0] + [
            entry / (exponent_index + 1) for exponent_index, entry in enumerate(coeffs)
        ]
        for row_number in range(node_count):
            running = 0.0
            for exponent_index in range(len(integral) - 1, -1, -1):
                running = running * points[row_number] + integral[exponent_index]
            node_table[row_number][column] = running
    return node_table


def sine_matrix(count):
    index = np.arange(1, count + 1)
    return math.sqrt(2.0 / (count + 1)) * np.sin(np.pi * np.outer(index, index) / (count + 1))


def eigenvalues(count):
    return 2.0 * np.cos(np.pi * np.arange(1, count + 1) / (count + 1))


def tables():
    coll = np.array(collocation_matrix(NODES))
    sx, sy, sz = (sine_matrix(n) for n in (GX, GY, NZ))
    kx = np.einsum("kx,fg->kfgx", sx, np.eye(8)).reshape(256, 256)
    n = np.arange(STEPS)
    real_dft = np.zeros((8, 2, STEPS))
    for q in range(8):
        real_dft[q, 0] = np.cos(2 * np.pi * q * n / STEPS)
        real_dft[q, 1] = -np.sin(2 * np.pi * q * n / STEPS) if q else np.cos(np.pi * n)
    shifted = np.zeros_like(real_dft)
    shifted[:, :, :-1] = real_dft[:, :, 1:]
    split = real_dft.reshape(8, 2, 8, 2)
    shifted = shifted.reshape(8, 2, 8, 2)
    nodes = np.eye(NODES).reshape(NODES, 2, 2)
    last = np.zeros((NODES, 2, 2))
    last[:, 1, 1] = 1.0
    two = np.eye(2)
    form = "qrsn,mtj,kl,zw->qkrmzstlnjw"
    mu0 = -np.einsum(form, split, nodes, two, two).reshape(256, 256)
    mu1 = np.einsum(form, shifted, last, two, two).reshape(256, 256)
    mf = np.einsum(form, split, coll.reshape(NODES, 2, 2), two, two).reshape(256, 256)
    mi = np.einsum("qrsn,mtj,kl,zw->stlnjwqkrmz", split, nodes, two, two).reshape(256, 256)
    zf = np.einsum("rp,mn,ksz->rmkspnz", two, np.eye(4), sz.reshape(NZ, 32, 2)).reshape(512, 512)
    lam_z, lam_x, lam_y = (eigenvalues(n) for n in (NZ, GX, GY))
    lam_xy = np.repeat(lam_x, 8)[:, None] + lam_y[None]
    lam_zy = lam_z[None, :, None] + lam_y.reshape(2, 1, 128)
    lam_x = np.broadcast_to(lam_x[:, None, None], (GX, 8, 128))
    start = np.linalg.solve(coll, np.ones(NODES))
    arrays = dict(sy=sy, kx=kx, lam_xy=lam_xy, mu0=mu0, mu1=mu1, mf=mf, zf=zf, zt=zf.T, mi=mi,
                  kt=kx.T, lam_zy=lam_zy, lam_x=lam_x)
    return coll, start, {k: np.asarray(v, np.float32) for k, v in arrays.items()}


COLL, START, TABLES = tables()
NAMES = tuple(TABLES)


def dot(a, b):
    return jnp.dot(a, b, precision=HIGH, preferred_element_type=jnp.float32)


def horner_tables(q, params, coef, tab, lam):
    partner = (16 - q) % 16 + 8 * ((8 - q) // 8)
    own = params[2 * (q // 2)] + params[2 * (q // 2) + 1]
    mate = params[2 * (partner // 2)] + params[2 * (partner // 2) + 1]
    row = lax.broadcasted_iota(jnp.int32, (8, 128), 0)
    odd = q % 2 == 1
    own = jnp.where(odd, pltpu.roll(own, 4, 0), own)
    mate = jnp.where(odd, mate, pltpu.roll(mate, 4, 0))
    x = jnp.where(row < 4, own, mate)
    bre, bim, mre, mim, dre, dim = [x if c == 0 else pltpu.roll(x, 128 - 16 * c, 1) for c in range(6)]
    pre, pim = bre * mre - bim * mim, bre * mim + bim * mre
    scale = 6.0 * DIFFUSION - REACTION
    ere, eim = 1.0 + scale * dre, scale * dim
    mag = ere * ere + eim * eim
    gre, gim = ere / mag, -eim / mag
    are, aim = DIFFUSION * dre, DIFFUSION * dim
    rre, rim = are * gre - aim * gim, are * gim + aim * gre
    first = q == 0
    for power in range(SWEEPS):
        tre, tim = pre * gre - pim * gim, pre * gim + pim * gre
        gre, gim = gre * rre - gim * rim, gre * rim + gim * rre
        kre, kim = (jnp.sum(v[0:4], axis=0, keepdims=True) for v in (tre, tim))
        ore, oim = (jnp.sum(v[4:8], axis=0, keepdims=True) for v in (tre, tim))
        both = kre + ore
        coef[0, power : power + 1, :] = jnp.where(first, kre, both)
        coef[1, power : power + 1, :] = jnp.where(first, 0.0, kim - oim)
        coef[2, power : power + 1, :] = jnp.where(first, ore, both)

    def entry(e, carry):
        following = []
        for a, c in enumerate(carry):
            col = jnp.broadcast_to(c[:, 0:1], (8, 128))
            acc = jnp.broadcast_to(col[SWEEPS - 1 : SWEEPS], (64, 128))
            for power in range(SWEEPS - 2, -1, -1):
                acc = acc * lam + col[power : power + 1]
            tab[a, e] = acc
            following.append(pltpu.roll(c, 127, 1))
        return tuple(following)

    lax.fori_loop(0, 16, entry, (coef[0], coef[1], coef[2]))


def pack_params(node, mix, back, shifts, out):
    row = lax.broadcasted_iota(jnp.int32, (8, 128), 0)
    lane = lax.broadcasted_iota(jnp.int32, (8, 128), 1)
    kind, i, j = lane // 16, (lane // 4) % 4, lane % 4
    k, m = row // 4, row % 4
    acc = jnp.zeros((8, 128), jnp.float32)
    for c in range(2):
        for kk in range(2):
            here = k == kk
            for l in range(2):
                mine = 2 * node + l
                at_mix = here & (kind == 2 + c) & (m == mine)
                at_back = here & (kind == c) & (i == mine)
                for n in range(4):
                    acc = jnp.where(at_mix & (j == n), mix[c, kk, l, n], acc)
                    acc = jnp.where(at_back & (m == n), back[c, kk, l, n], acc)
                acc = jnp.where(here & (kind == 4 + c) & (m == mine), shifts[c, kk, l], acc)
    out[...] = acc


def kernel(u_hbm, init_hbm, alpha_ref, mix_ref, back_ref, shifts_ref, *refs):
    consts = dict(zip(NAMES, refs[: len(NAMES)]))
    refs = refs[len(NAMES) :]
    out_u, out_r = refs[:2]
    refs = refs[2:]
    held = dict(zip(NAMES, refs[: len(NAMES)]))
    refs = refs[len(NAMES) :]
    (u_ref, init_ref, su, ru, sf, rf, sp, rp, s2, r2, s3, r3, s4, r4, halo, grid, ub, wb, whalo, before, coef, tab,
     sw, ow, load_sem, send_sem, recv_sem) = refs
    step, node, space = (lax.axis_index(a) for a in ("step", "node", "space"))
    me = step * 2 + node

    load_u = pltpu.make_async_copy(u_hbm, u_ref, load_sem.at[len(NAMES)])
    load_init = pltpu.make_async_copy(init_hbm, init_ref, load_sem.at[len(NAMES) + 1])
    load_u.start()
    loads = {}
    for index, name in enumerate(NAMES):
        loads[name] = pltpu.make_async_copy(consts[name], held[name], load_sem.at[index])
        loads[name].start()
    load_init.start()

    def get(name):
        loads[name].wait()
        return held[name]

    barrier = pltpu.get_barrier_semaphore()

    def group_id(d):
        other = (me + d) % 16
        return other, {"step": other // 2, "node": other % 2}

    def greet_group(d, _):
        pl.semaphore_signal(barrier, inc=1, device_id=group_id(d)[1])
        return 0

    def greet_space(d, _):
        pl.semaphore_signal(barrier, inc=1, device_id={"space": (space + d) % 32})
        return 0

    lax.fori_loop(1, 16, greet_group, 0)
    lax.fori_loop(1, 32, greet_space, 0)
    pl.semaphore_wait(barrier, 46)

    def remote(src, dst, sem, device):
        return pltpu.make_async_remote_copy(
            src_ref=src, dst_ref=dst, send_sem=send_sem.at[sem], recv_sem=recv_sem.at[sem], device_id=device
        )

    up, down = {"space": (space + 1) % 32}, {"space": (space + 31) % 32}
    HALO_UP, HALO_DOWN, GROUP_U, GROUP_F, PARAMS, SPACE, BACK, CORR, OTHER, W_UP, W_DOWN, BEFORE = range(12)
    pending = [
        remote(u_hbm.at[:, 1], halo.at[0], HALO_UP, up),
        remote(u_hbm.at[:, 0], halo.at[1], HALO_DOWN, down),
    ]
    for copy in pending:
        copy.start()

    def to_group(src, dst, sem):
        def body(d, _):
            other, device = group_id(d)
            remote(src.at[other], dst.at[me], sem, device).start()
            return 0
        lax.fori_loop(1, 16, body, 0)
        dst[me] = src[me]

    def to_space(src, dst, sem):
        def body(d, _):
            other = (space + d) % 32
            remote(src.at[other], dst.at[space], sem, {"space": other}).start()
            return 0
        lax.fori_loop(1, 32, body, 0)
        dst[space] = src[space]

    def arrived(ref, sem, count):
        part = ref.at[pl.ds(0, count)]
        remote(part, part, sem, up).wait_recv()

    def sent(ref, sem, count):
        part = ref.at[pl.ds(0, count)]
        remote(part, part, sem, up).wait_send()

    load_u.wait()
    sy, kx = get("sy"), get("kx")
    uh = dot(kx[...], dot(u_ref[...].reshape(256, 256), sy[...]))
    su[...] = uh.reshape(16, 16, 256)
    to_group(su, ru, GROUP_U)

    low = jnp.where(space == 0, 0.0, DIFFUSION)
    high = jnp.where(space == 31, 0.0, DIFFUSION)
    begin = [
        jnp.where(step == 0, jnp.where(node == 0, START[m], START[2 + m]), 0.0).astype(jnp.float32) for m in range(2)
    ]
    load_init.wait()
    pending[0].wait_recv()
    pending[1].wait_recv()
    for nm in range(4):
        for z in range(2):
            u = u_ref[nm, z]
            beside = DIFFUSION * u_ref[nm, 1 - z] + (low if z == 0 else high) * halo[z, nm]
            value = beside - (6.0 * DIFFUSION - REACTION) * u - REACTION * (u * u * u)
            if nm < 2:
                value = value + begin[nm] * init_ref[z]
            grid[nm * 2 + z] = value
    fh = dot(kx[...], dot(grid[...].reshape(256, 256), sy[...]))
    fh = fh + DIFFUSION * get("lam_xy")[...] * su[...].reshape(256, 256)
    sf[...] = fh.reshape(16, 16, 256)
    to_group(sf, rf, GROUP_F)

    pack_params(node, mix_ref, back_ref, shifts_ref, sp)

    def send_params(d, _):
        remote(sp, rp.at[me], PARAMS, group_id(d)[1]).start()
        return 0

    lax.fori_loop(1, 16, send_params, 0)
    rp[me] = sp[...]

    rate = alpha_ref[0].astype(jnp.float32) * (math.log(2.0) / 16.0 / STEPS)
    col = lax.broadcasted_iota(jnp.int32, (1, 256), 1)
    when = (2 * (col // 32) + (col // 4) % 2).astype(jnp.float32)
    scale0, scale1 = jnp.exp(-rate * when), jnp.exp(-rate * (when + 1.0))
    mu = get("mu0")[...] * scale0 + get("mu1")[...] * scale1
    mf = get("mf")[...] * scale0
    arrived(ru, GROUP_U, 15)
    spec = dot(mu, ru[...].reshape(256, 256))
    arrived(rf, GROUP_F, 15)
    spec = spec + dot(mf, rf[...].reshape(256, 256))
    for h in range(2):
        s2[:, h] = spec[:, h * 128 : h * 128 + 128].reshape(16, 16, 128)
    s2_flat, r2_flat = s2.reshape(32, 16, 128), r2
    to_space(s2_flat, r2_flat, SPACE)
    other_u = remote(u_hbm, ub.at[node], OTHER, {"node": 1 - node})
    other_u.start()
    ub[node] = u_ref[...]

    arrived(rp, PARAMS, 15)
    q = space // 4
    lam = get("lam_zy")[space % 2] + jnp.broadcast_to(
        get("lam_x")[2 * me + (space // 2) % 2][0:1], (64, 128))
    horner_tables(q, rp, coef, tab, lam)
    row = lax.broadcasted_iota(jnp.int32, (256, 256), 0)
    when = (2 * (row // 32) + (row // 4) % 2).astype(jnp.float32)
    held["mi"][...] = get("mi")[...] * (jnp.exp(rate * when) * (1.0 / STEPS))

    zf, zt = get("zf"), get("zt")
    arrived(r2_flat, SPACE, 31)
    sw[...] = dot(zf[...], r2[...].reshape(512, 128)).reshape(8, 64, 128)

    def solve(z, _):
        at = pl.ds(pl.multiple_of(z * 8, 8), 8)
        s = [sw[i, at, :] for i in range(8)]
        for i in range(4):
            re = im = None
            for j in range(4):
                a, e, d = (tab[c, 4 * i + j, at, :] for c in range(3))
                tre, tim = a * s[j] - e * s[4 + j], e * s[j] + d * s[4 + j]
                re, im = (tre, tim) if re is None else (re + tre, im + tim)
            ow[i, at, :] = re
            ow[4 + i, at, :] = im
        return 0

    lax.fori_loop(0, 8, solve, 0)
    s3[...] = dot(zt[...], ow[...].reshape(512, 128)).reshape(32, 16, 128)
    to_space(s3, r3, BACK)
    kt = get("kt")
    arrived(r3, BACK, 31)
    for h in range(2):
        part = r3[...].reshape(16, 2, 16, 128)[:, h].reshape(256, 128)
        s4[:, :, :, h * 128 : h * 128 + 128] = dot(held["mi"][...], part).reshape(8, 2, 16, 128)

    def send_corr(d, _):
        other, device = group_id(d)
        remote(s4.at[other // 2], r4.at[:, me], CORR, device).start()
        return 0

    lax.fori_loop(1, 16, send_corr, 0)
    r4[:, me] = s4[step]
    other_u.wait_recv()
    whole = r4.at[:, pl.ds(0, 15)]
    remote(whole, whole, CORR, up).wait_recv()
    for g in range(2):
        d = dot(dot(kt[...], r4[g].reshape(256, 256)), sy[...])
        ub[g] = ub[g] + d.reshape(4, 2, 32, 256)
    out_u[...] = ub[node]

    weight = [
        [jnp.where(node == 0, COLL[m][j], COLL[2 + m][j]).astype(jnp.float32) for j in range(4)] for m in range(2)
    ]

    def nodes_at(n, z):
        return [ub[j // 2, 2 * n + j % 2, z] for j in range(4)]

    for n in range(2):
        for z in range(2):
            u = nodes_at(n, z)
            for m in range(2):
                wb[2 * n + m, z] = sum(weight[m][j] * u[j] for j in range(4))
    last = [
        remote(wb.at[:, 1], whalo.at[0], W_UP, up),
        remote(wb.at[:, 0], whalo.at[1], W_DOWN, down),
        remote(ub.at[1, 3], before, BEFORE, {"step": (step + 1) % 8}),
    ]
    for copy in last:
        copy.start()
    x = lax.broadcasted_iota(jnp.int32, (32, 256), 0)
    y = lax.broadcasted_iota(jnp.int32, (32, 256), 1)
    for n in range(2):
        for z in range(2):
            cubes = [v * v * v for v in nodes_at(n, z)]
            for m in range(2):
                w = wb[2 * n + m, z]
                beside = (
                    wb[2 * n + m, 1 - z]
                    + jnp.where(x == 0, 0.0, pltpu.roll(w, 1, 0))
                    + jnp.where(x == 31, 0.0, pltpu.roll(w, 31, 0))
                    + jnp.where(y == 0, 0.0, pltpu.roll(w, 1, 1))
                    + jnp.where(y == 255, 0.0, pltpu.roll(w, 255, 1))
                )
                value = DIFFUSION * beside - (6.0 * DIFFUSION - REACTION) * w
                value = value - REACTION * sum(weight[m][j] * cubes[j] for j in range(4)) - ub[node, 2 * n + m, z]
                if n == 1:
                    value = value + ub[1, 1, z]
                out_r[2 * n + m, z] = value
    for copy in last:
        copy.wait_recv()
    for z in range(2):
        opening = jnp.where(step == 0, init_ref[z], before[z])
        for nm in range(4):
            edge = (low if z == 0 else high) * whalo[z, nm]
            out_r[nm, z] = out_r[nm, z] + (edge + opening if nm < 2 else edge)

    for copy in pending + last + [other_u]:
        copy.wait_send()
    sent(su, GROUP_U, 15)
    sent(sf, GROUP_F, 15)
    sent(rp, PARAMS, 15)
    sent(s3, SPACE, 31)
    sent(s3, BACK, 31)
    remote(whole, whole, CORR, up).wait_send()


def on_device(iterate, initial_value, alpha_power, node_mix, node_back, shifts):
    consts = [jnp.asarray(TABLES[name]) for name in NAMES]
    f32 = jnp.float32
    vmem = lambda *shape: pltpu.VMEM(shape, f32)
    block = jax.ShapeDtypeStruct((4, 2, 32, 256), f32)
    in_vmem, in_smem, in_any = (pl.BlockSpec(memory_space=m) for m in (pltpu.VMEM, pltpu.SMEM, pl.ANY))
    updated, residual = pl.pallas_call(
        kernel,
        out_shape=(block, block),
        in_specs=[in_any] * 2 + [in_smem] * 4 + [in_any] * len(NAMES),
        out_specs=(in_vmem, in_vmem),
        scratch_shapes=[vmem(*TABLES[name].shape) for name in NAMES]
        + [vmem(4, 2, 32, 256), vmem(2, 32, 256)]
        + [vmem(16, 16, 256)] * 4
        + [vmem(8, 128), vmem(16, 8, 128)]
        + [vmem(16, 2, 16, 128), vmem(32, 16, 128)]
        + [vmem(32, 16, 128)] * 2
        + [vmem(8, 2, 16, 256), vmem(2, 16, 16, 256)]
        + [vmem(2, 4, 32, 256), vmem(8, 32, 256)]
        + [vmem(2, 4, 2, 32, 256), vmem(4, 2, 32, 256), vmem(2, 4, 32, 256), vmem(2, 32, 256)]
        + [vmem(3, 8, 128), vmem(3, 16, 64, 128)]
        + [vmem(8, 64, 128)] * 2
        + [pltpu.SemaphoreType.DMA((len(NAMES) + 2,)), pltpu.SemaphoreType.DMA((12,)), pltpu.SemaphoreType.DMA((12,))],
        compiler_params=pltpu.CompilerParams(
            collective_id=0, has_side_effects=True, vmem_limit_bytes=63 * 1024 * 1024
        ),
    )(iterate.reshape(4, 2, 32, 256), initial_value, alpha_power, node_mix, node_back, shifts, *consts)
    return updated.reshape(iterate.shape), residual.reshape(iterate.shape)


def solution(mesh):
    in_specs = (
        P("step", "node", "space", None, None),
        P("space", None, None),
        P(),
        P(None, "step", "node", None),
        P(None, "step", "node", None),
        P(None, "step", "node"),
    )
    out_specs = (P("step", "node", "space", None, None), P("step", "node", "space", None, None))
    return jax.shard_map(
        on_device, mesh=mesh, in_specs=in_specs, out_specs=out_specs, check_vma=False
    )
```

```python
import math

import jax
import jax.numpy as jnp
import ml_dtypes
import numpy as np
from jax import lax
from jax.experimental import pallas as pl
from jax.experimental.pallas import tpu as pltpu
from jax.sharding import PartitionSpec as P

STEPS = 16
NODES = 4
SWEEPS = 8
GX = 32
GY = 256
NZ = 64

DIFFUSION = 0.5
REACTION = 1.0


def legendre_pair(degree, point):
    previous_term, current_term = (1.0, point)
    for degree_now in range(1, degree):
        previous_term, current_term = (
            current_term,
            ((2 * degree_now + 1) * point * current_term - degree_now * previous_term)
            / (degree_now + 1),
        )
    return (current_term, previous_term)


def radau_value(count, point):
    high_term, low_term = legendre_pair(count, point)
    return high_term - low_term


def radau_points(count):
    roots_found = []
    samples = 4000
    for sample_index in range(samples):
        left_end = -1.0 + 2.0 * sample_index / samples
        right_end = -1.0 + 2.0 * (sample_index + 1) / samples
        if radau_value(count, left_end) * radau_value(count, right_end) < 0.0:
            for halving in range(200):
                middle = 0.5 * (left_end + right_end)
                if radau_value(count, left_end) * radau_value(count, middle) <= 0.0:
                    right_end = middle
                else:
                    left_end = middle
            roots_found.append(0.5 * (left_end + right_end))
    roots_found.append(1.0)
    return [(root_value + 1.0) / 2.0 for root_value in roots_found]


def collocation_matrix(node_count):
    points = radau_points(node_count)
    node_table = [[0.0] * node_count for row_number in range(node_count)]
    for column in range(node_count):
        coeffs = [1.0]
        for another in range(node_count):
            if another != column:
                spacing = points[column] - points[another]
                raised = [0.0] + coeffs
                lowered = [entry * points[another] for entry in coeffs] + [0.0]
                coeffs = [
                    (first_entry - second_entry) / spacing
                    for first_entry, second_entry in zip(raised, lowered)
                ]
        integral = [0.0] + [
            entry / (exponent_index + 1) for exponent_index, entry in enumerate(coeffs)
        ]
        for row_number in range(node_count):
            running = 0.0
            for exponent_index in range(len(integral) - 1, -1, -1):
                running = running * points[row_number] + integral[exponent_index]
            node_table[row_number][column] = running
    return node_table


def sine_matrix(count):
    index = np.arange(1, count + 1)
    return math.sqrt(2.0 / (count + 1)) * np.sin(np.pi * np.outer(index, index) / (count + 1))


def eigenvalues(count):
    return 2.0 * np.cos(np.pi * np.arange(1, count + 1) / (count + 1))


def tables():
    coll = np.array(collocation_matrix(NODES))
    sx, sy, sz = (sine_matrix(n) for n in (GX, GY, NZ))
    lam_z, lam_x, lam_y = (eigenvalues(n) for n in (NZ, GX, GY))
    kx = np.einsum("pcx,fg->cpfgx", sx.reshape(16, 2, GX), np.eye(8)).reshape(2, 128, 256)
    n = np.arange(STEPS)
    real_dft = np.zeros((8, 2, STEPS))
    for q in range(8):
        real_dft[q, 0] = np.cos(2 * np.pi * q * n / STEPS)
        real_dft[q, 1] = -np.sin(2 * np.pi * q * n / STEPS) if q else np.cos(np.pi * n)
    shifted = np.zeros_like(real_dft)
    shifted[:, :, :-1] = real_dft[:, :, 1:]
    split = real_dft.reshape(8, 2, 8, 2)
    shifted = shifted.reshape(8, 2, 8, 2)
    nodes = np.eye(NODES).reshape(NODES, 2, 2)
    last = np.zeros((NODES, 2, 2))
    last[:, 1, 1] = 1.0
    two = np.eye(2)
    form = "qrsn,mtj,zw->qrmzstnjw"
    m0 = np.zeros((128, 2, 128))
    m1 = np.zeros((128, 2, 128))
    m0[:, 0] = -np.einsum(form, split, nodes, two).reshape(128, 128)
    m0[:, 1] = np.einsum(form, split, coll.reshape(NODES, 2, 2), two).reshape(128, 128)
    m1[:, 0] = np.einsum(form, shifted, last, two).reshape(128, 128)
    m0, m1 = m0.reshape(128, 256), m1.reshape(128, 256)
    mi = np.einsum("qrsn,mtj,zw->stnjwqrmz", split, nodes, two).reshape(128, 128)
    zf = np.einsum("mn,ksz->mksnz", np.eye(4), sz.reshape(NZ, 32, 2)).reshape(256, 256)
    lam_xy = lam_x.reshape(16, 2).T[:, :, None, None] + lam_y
    lam_xy = np.broadcast_to(lam_xy, (2, 16, 8, 256)).reshape(2, 128, 256)
    lam_zy = lam_z[None, :, None] + lam_y.reshape(2, 1, 128)
    lam_x = np.broadcast_to(lam_x[:, None, None], (GX, 8, 128))
    start = np.linalg.solve(coll, np.ones(NODES))
    exact = dict(lam_xy=lam_xy, m0=m0, m1=m1, mi=mi, lam_zy=lam_zy, lam_x=lam_x)
    arrays = dict(sy=halves(sy), kx=halves(kx))
    arrays.update({k: np.asarray(v, np.float32) for k, v in exact.items()})
    kt = kx.transpose(0, 2, 1)
    arrays.update(zf=halves(zf), zt=halves(zf.T), kt=halves(kt))
    return coll, start, arrays


def halves(matrix):
    matrix = np.asarray(matrix, np.float32)
    upper = matrix.astype(ml_dtypes.bfloat16)
    lower = (matrix - upper.astype(np.float32)).astype(ml_dtypes.bfloat16)
    return np.stack([upper, lower])


COLL, START, TABLES = tables()
NAMES = tuple(TABLES)


def parts(x):
    upper = x.astype(jnp.bfloat16)
    return upper, (x - upper.astype(jnp.float32)).astype(jnp.bfloat16)


def dot3(a, b):
    one = lambda x, y: jnp.dot(x, y, preferred_element_type=jnp.float32)
    return one(a[0], b[0]) + (one(a[0], b[1]) + one(a[1], b[0]))


def horner_tables(q, params, coef, tab, lam):
    partner = (16 - q) % 16 + 8 * ((8 - q) // 8)
    own = params[2 * (q // 2)] + params[2 * (q // 2) + 1]
    mate = params[2 * (partner // 2)] + params[2 * (partner // 2) + 1]
    row = lax.broadcasted_iota(jnp.int32, (8, 128), 0)
    odd = q % 2 == 1
    own = jnp.where(odd, pltpu.roll(own, 4, 0), own)
    mate = jnp.where(odd, mate, pltpu.roll(mate, 4, 0))
    x = jnp.where(row < 4, own, mate)
    bre, bim, mre, mim, dre, dim = [x if c == 0 else pltpu.roll(x, 128 - 16 * c, 1) for c in range(6)]
    pre, pim = bre * mre - bim * mim, bre * mim + bim * mre
    scale = 6.0 * DIFFUSION - REACTION
    ere, eim = 1.0 + scale * dre, scale * dim
    mag = ere * ere + eim * eim
    gre, gim = ere / mag, -eim / mag
    are, aim = DIFFUSION * dre, DIFFUSION * dim
    rre, rim = are * gre - aim * gim, are * gim + aim * gre
    first = q == 0
    for power in range(SWEEPS):
        tre, tim = pre * gre - pim * gim, pre * gim + pim * gre
        gre, gim = gre * rre - gim * rim, gre * rim + gim * rre
        kre, kim = (jnp.sum(v[0:4], axis=0, keepdims=True) for v in (tre, tim))
        ore, oim = (jnp.sum(v[4:8], axis=0, keepdims=True) for v in (tre, tim))
        both = kre + ore
        coef[0, power : power + 1, :] = jnp.where(first, kre, both)
        coef[1, power : power + 1, :] = jnp.where(first, 0.0, kim - oim)
        coef[2, power : power + 1, :] = jnp.where(first, ore, both)

    def entry(e, carry):
        following = []
        for a, c in enumerate(carry):
            col = jnp.broadcast_to(c[:, 0:1], (8, 128))
            acc = jnp.broadcast_to(col[SWEEPS - 1 : SWEEPS], (64, 128))
            for power in range(SWEEPS - 2, -1, -1):
                acc = acc * lam + col[power : power + 1]
            tab[a, e] = acc
            following.append(pltpu.roll(c, 127, 1))
        return tuple(following)

    lax.fori_loop(0, 16, entry, (coef[0], coef[1], coef[2]))


def pack_params(node, mix, back, shifts, out):
    row = lax.broadcasted_iota(jnp.int32, (8, 128), 0)
    lane = lax.broadcasted_iota(jnp.int32, (8, 128), 1)
    kind, i, j = lane // 16, (lane // 4) % 4, lane % 4
    k, m = row // 4, row % 4
    acc = jnp.zeros((8, 128), jnp.float32)
    for c in range(2):
        for kk in range(2):
            here = k == kk
            for l in range(2):
                mine = 2 * node + l
                at_mix = here & (kind == 2 + c) & (m == mine)
                at_back = here & (kind == c) & (i == mine)
                for n in range(4):
                    acc = jnp.where(at_mix & (j == n), mix[c, kk, l, n], acc)
                    acc = jnp.where(at_back & (m == n), back[c, kk, l, n], acc)
                acc = jnp.where(here & (kind == 4 + c) & (m == mine), shifts[c, kk, l], acc)
    out[...] = acc


def kernel(u_hbm, init_hbm, alpha_ref, mix_ref, back_ref, shifts_ref, *refs):
    consts = dict(zip(NAMES, refs[: len(NAMES)]))
    refs = refs[len(NAMES) :]
    out_u, out_r = refs[:2]
    refs = refs[2:]
    held = dict(zip(NAMES, refs[: len(NAMES)]))
    refs = refs[len(NAMES) :]
    (u_ref, init_ref, su, sf, r1, sp, rp, s2, r2, s3, r3, s4, r4, halo, grid, ub, wb, whalo, before, coef, tab,
     mm, mb, sw, ow, load_sem, send_sem, recv_sem) = refs
    step, node, space = (lax.axis_index(a) for a in ("step", "node", "space"))
    me = step * 2 + node
    q, chunk, half = space // 4, (space // 2) % 2, space % 2

    load_u = pltpu.make_async_copy(u_hbm, u_ref, load_sem.at[len(NAMES)])
    load_init = pltpu.make_async_copy(init_hbm, init_ref, load_sem.at[len(NAMES) + 1])
    load_u.start()
    loads = {}
    for index, name in enumerate(NAMES):
        loads[name] = pltpu.make_async_copy(consts[name], held[name], load_sem.at[index])
        loads[name].start()
    load_init.start()

    def get(name):
        loads[name].wait()
        return held[name]

    barrier = pltpu.get_barrier_semaphore()

    def group_id(d):
        other = (me + d) % 16
        return other, {"step": other // 2, "node": other % 2}

    def greet_group(d, _):
        pl.semaphore_signal(barrier, inc=1, device_id=group_id(d)[1])
        return 0

    def greet_space(d, _):
        pl.semaphore_signal(barrier, inc=1, device_id={"space": (space + d) % 32})
        return 0

    lax.fori_loop(1, 16, greet_group, 0)
    lax.fori_loop(1, 32, greet_space, 0)

    load_u.wait()
    get("sy"), get("kx")
    sy = (held["sy"][0], held["sy"][1])

    def to_sines(field):
        return parts(dot3(parts(field), sy))

    def x_sines(c, rows):
        return dot3((held["kx"][0, c], held["kx"][1, c]), rows)

    rows = to_sines(u_ref[...].reshape(256, 256))
    for c in range(2):
        su[c] = x_sines(c, rows).reshape(16, 8, 256)
    pl.semaphore_wait(barrier, 46)

    def remote(src, dst, sem, device, recv=None):
        recv = sem if recv is None else recv
        return pltpu.make_async_remote_copy(
            src_ref=src, dst_ref=dst, send_sem=send_sem.at[sem], recv_sem=recv_sem.at[recv], device_id=device
        )

    up, down = {"space": (space + 1) % 32}, {"space": (space + 31) % 32}
    HALO_UP, HALO_DOWN, OTHER, PARAMS, SPACE, W_UP, W_DOWN, BEFORE = range(8)
    FIELD, FORCE, BACK, CORR = 8, 10, 12, 14
    pending = [
        remote(u_hbm.at[:, 1], halo.at[0], HALO_UP, up),
        remote(u_hbm.at[:, 0], halo.at[1], HALO_DOWN, down),
    ]
    for copy in pending:
        copy.start()

    def to_group(src, dst, sem):
        def body(d, _):
            other, device = group_id(d)
            remote(src.at[other], dst.at[me], sem, device).start()
            return 0

        lax.fori_loop(1, 16, body, 0)
        dst[me] = src[me]

    def block_of(ref, count):
        return ref.at[pl.ds(0, count)]

    def arrived(ref, sem, count):
        part = block_of(ref, count)
        remote(part, part, sem, up).wait_recv()

    def sent(ref, sem, count):
        part = block_of(ref, count)
        remote(part, part, sem, up).wait_send()

    for c in range(2):
        to_group(su.at[c], r1.at[c, 0], FIELD + c)

    pack_params(node, mix_ref, back_ref, shifts_ref, sp)

    def send_params(d, _):
        remote(sp, rp.at[me], PARAMS, group_id(d)[1]).start()
        return 0

    rate = alpha_ref[0].astype(jnp.float32) * (math.log(2.0) / 16.0 / STEPS)
    col = lax.broadcasted_iota(jnp.int32, (1, 256), 1) % 128
    when = (2 * (col // 16) + (col // 4) % 2).astype(jnp.float32)
    scaled = get("m0")[...] * jnp.exp(-rate * when) + get("m1")[...] * jnp.exp(-rate * (when + 1.0))
    mm[0], mm[1] = parts(scaled)
    row = lax.broadcasted_iota(jnp.int32, (128, 128), 0)
    when = (2 * (row // 16) + (row // 4) % 2).astype(jnp.float32)
    mb[0], mb[1] = parts(get("mi")[...] * (jnp.exp(rate * when) * (1.0 / STEPS)))

    low = jnp.where(space == 0, 0.0, DIFFUSION)
    high = jnp.where(space == 31, 0.0, DIFFUSION)
    begin = [
        jnp.where(step == 0, jnp.where(node == 0, START[m], START[2 + m]), 0.0).astype(jnp.float32) for m in range(2)
    ]
    load_init.wait()
    get("lam_xy")
    pending[0].wait_recv()
    pending[1].wait_recv()
    for nm in range(4):
        for z in range(2):
            u = u_ref[nm, z]
            beside = DIFFUSION * u_ref[nm, 1 - z] + (low if z == 0 else high) * halo[z, nm]
            value = beside - (6.0 * DIFFUSION - REACTION) * u - REACTION * (u * u * u)
            if nm < 2:
                value = value + begin[nm] * init_ref[z]
            grid[nm * 2 + z] = value
    rows = to_sines(grid[...].reshape(256, 256))
    for c in range(2):
        value = x_sines(c, rows) + DIFFUSION * held["lam_xy"][c] * su[c].reshape(128, 256)
        sf[c] = value.reshape(16, 8, 256)
        to_group(sf.at[c], r1.at[c, 1], FORCE + c)
    lax.fori_loop(1, 16, send_params, 0)
    rp[me] = sp[...]

    for c in range(2):
        arrived(r1.at[c, 0], FIELD + c, 15)
        arrived(r1.at[c, 1], FORCE + c, 15)
        spec = dot3((mm[0], mm[1]), parts(r1[c].reshape(256, 256))).reshape(8, 2, 8, 256)
        for h in range(2):
            for part in range(2):
                s2[c, h, :, :, part * 128 : part * 128 + 128] = spec[:, part, :, h * 128 : h * 128 + 128]
        for h in range(2):
            def send_spec(d, _):
                other = (q + d) % 8
                place = 4 * other + 2 * c + h
                @pl.when(place != space)
                def _():
                    remote(s2.at[c, h, other], r2.at[space], SPACE, {"space": place}).start()
                return 0

            lax.fori_loop(0, 8, send_spec, 0)
    r2[space] = s2[chunk, half, q]
    other_u = remote(u_hbm, ub.at[node], OTHER, {"node": 1 - node})
    other_u.start()
    ub[node] = u_ref[...]

    arrived(rp, PARAMS, 15)
    lam = get("lam_zy")[half] + jnp.broadcast_to(get("lam_x")[2 * me + chunk][0:1], (64, 128))
    horner_tables(q, rp, coef, tab, lam)
    get("zf"), get("zt")
    arrived(r2, SPACE, 31)
    sw[...] = dot3((held["zf"][0], held["zf"][1]), parts(r2[...].reshape(256, 256))).reshape(4, 64, 256)

    def solve(z, _):
        at = pl.ds(pl.multiple_of(z * 8, 8), 8)
        re_in = [sw[i, at, 0:128] for i in range(4)]
        im_in = [sw[i, at, 128:256] for i in range(4)]
        for i in range(4):
            re = im = None
            for j in range(4):
                a, e, d = (tab[c, 4 * i + j, at, :] for c in range(3))
                tre, tim = a * re_in[j] - e * im_in[j], e * re_in[j] + d * im_in[j]
                re, im = (tre, tim) if re is None else (re + tre, im + tim)
            ow[i, at, 0:128] = re
            ow[i, at, 128:256] = im
        return 0

    lax.fori_loop(0, 8, solve, 0)
    value = dot3((held["zt"][0], held["zt"][1]), parts(ow[...].reshape(256, 256))).reshape(32, 8, 256)
    for part in range(2):
        s3[:, part] = value[:, :, part * 128 : part * 128 + 128]

    def send_back(d, _):
        other = (space + d) % 32
        remote(s3.at[other], r3.at[chunk, half, q], BACK, {"space": other}, BACK + chunk).start()
        return 0

    lax.fori_loop(1, 32, send_back, 0)
    r3[chunk, half, q] = s3[space]
    get("kt")
    for c in range(2):
        for here in range(2):
            @pl.when((chunk == c) if here else (chunk != c))
            def _():
                part = block_of(s3, 16 - here)
                remote(part, part, BACK, up, BACK + c).wait_recv()
        for h in range(2):
            value = dot3((mb[0], mb[1]), parts(r3[c, h].reshape(128, 128)))
            s4[c, :, :, :, h * 128 : h * 128 + 128] = value.reshape(8, 2, 8, 128)

        def send_corr(d, _):
            other, device = group_id(d)
            remote(s4.at[c, other // 2], r4.at[c, :, me], CORR + c, device).start()
            return 0

        lax.fori_loop(1, 16, send_corr, 0)
        r4[c, :, me] = s4[c, step]
    other_u.wait_recv()
    for c in range(2):
        whole = r4.at[c, :, pl.ds(0, 15)]
        remote(whole, whole, CORR + c, up).wait_recv()
        for g in range(2):
            rows = to_sines(r4[c, g].reshape(128, 256))
            d = dot3((held["kt"][0, c], held["kt"][1, c]), rows)
            ub[g] = ub[g] + d.reshape(4, 2, 32, 256)
    out_u[...] = ub[node]

    weight = [
        [jnp.where(node == 0, COLL[m][j], COLL[2 + m][j]).astype(jnp.float32) for j in range(4)] for m in range(2)
    ]

    def nodes_at(n, z):
        return [ub[j // 2, 2 * n + j % 2, z] for j in range(4)]

    for n in range(2):
        for z in range(2):
            u = nodes_at(n, z)
            for m in range(2):
                wb[2 * n + m, z] = sum(weight[m][j] * u[j] for j in range(4))
    last = [
        remote(wb.at[:, 1], whalo.at[0], W_UP, up),
        remote(wb.at[:, 0], whalo.at[1], W_DOWN, down),
        remote(ub.at[1, 3], before, BEFORE, {"step": (step + 1) % 8}),
    ]
    for copy in last:
        copy.start()
    x = lax.broadcasted_iota(jnp.int32, (32, 256), 0)
    y = lax.broadcasted_iota(jnp.int32, (32, 256), 1)
    for n in range(2):
        for z in range(2):
            cubes = [v * v * v for v in nodes_at(n, z)]
            for m in range(2):
                w = wb[2 * n + m, z]
                beside = (
                    wb[2 * n + m, 1 - z]
                    + jnp.where(x == 0, 0.0, pltpu.roll(w, 1, 0))
                    + jnp.where(x == 31, 0.0, pltpu.roll(w, 31, 0))
                    + jnp.where(y == 0, 0.0, pltpu.roll(w, 1, 1))
                    + jnp.where(y == 255, 0.0, pltpu.roll(w, 255, 1))
                )
                value = DIFFUSION * beside - (6.0 * DIFFUSION - REACTION) * w
                value = value - REACTION * sum(weight[m][j] * cubes[j] for j in range(4)) - ub[node, 2 * n + m, z]
                if n == 1:
                    value = value + ub[1, 1, z]
                out_r[2 * n + m, z] = value
    for copy in last:
        copy.wait_recv()
    for z in range(2):
        opening = jnp.where(step == 0, init_ref[z], before[z])
        for nm in range(4):
            edge = (low if z == 0 else high) * whalo[z, nm]
            out_r[nm, z] = out_r[nm, z] + (edge + opening if nm < 2 else edge)

    for copy in pending + last + [other_u]:
        copy.wait_send()
    for c in range(2):
        sent(su.at[c], FIELD + c, 15)
        sent(sf.at[c], FORCE + c, 15)
        whole = r4.at[c, :, pl.ds(0, 15)]
        remote(whole, whole, CORR + c, up).wait_send()
    sent(rp, PARAMS, 15)
    sent(r2, SPACE, 31)
    sent(s3, BACK, 31)


def on_device(iterate, initial_value, alpha_power, node_mix, node_back, shifts):
    consts = [jnp.asarray(TABLES[name]) for name in NAMES]
    f32 = jnp.float32
    vmem = lambda *shape: pltpu.VMEM(shape, f32)
    block = jax.ShapeDtypeStruct((4, 2, 32, 256), f32)
    in_vmem, in_smem, in_any = (pl.BlockSpec(memory_space=m) for m in (pltpu.VMEM, pltpu.SMEM, pl.ANY))
    updated, residual = pl.pallas_call(
        kernel,
        out_shape=(block, block),
        in_specs=[in_any] * 2 + [in_smem] * 4 + [in_any] * len(NAMES),
        out_specs=(in_vmem, in_vmem),
        scratch_shapes=[pltpu.VMEM(TABLES[name].shape, TABLES[name].dtype) for name in NAMES]
        + [vmem(4, 2, 32, 256), vmem(2, 32, 256)]
        + [vmem(2, 16, 8, 256)] * 2
        + [vmem(2, 2, 16, 8, 256)]
        + [vmem(8, 128), vmem(16, 8, 128)]
        + [vmem(2, 2, 8, 8, 256), vmem(32, 8, 256)]
        + [vmem(32, 2, 8, 128), vmem(2, 2, 8, 2, 8, 128)]
        + [vmem(2, 8, 2, 8, 256), vmem(2, 2, 16, 8, 256)]
        + [vmem(2, 4, 32, 256), vmem(8, 32, 256)]
        + [vmem(2, 4, 2, 32, 256), vmem(4, 2, 32, 256), vmem(2, 4, 32, 256), vmem(2, 32, 256)]
        + [vmem(3, 8, 128), vmem(3, 16, 64, 128)]
        + [pltpu.VMEM((2, 128, 256), jnp.bfloat16), pltpu.VMEM((2, 128, 128), jnp.bfloat16)]
        + [vmem(4, 64, 256)] * 2
        + [pltpu.SemaphoreType.DMA((len(NAMES) + 2,)), pltpu.SemaphoreType.DMA((16,)), pltpu.SemaphoreType.DMA((16,))],
        compiler_params=pltpu.CompilerParams(
            collective_id=0, has_side_effects=True, vmem_limit_bytes=63 * 1024 * 1024
        ),
    )(iterate.reshape(4, 2, 32, 256), initial_value, alpha_power, node_mix, node_back, shifts, *consts)
    return updated.reshape(iterate.shape), residual.reshape(iterate.shape)


def solution(mesh):
    in_specs = (
        P("step", "node", "space", None, None),
        P("space", None, None),
        P(),
        P(None, "step", "node", None),
        P(None, "step", "node", None),
        P(None, "step", "node"),
    )
    out_specs = (P("step", "node", "space", None, None), P("step", "node", "space", None, None))
    return jax.shard_map(
        on_device, mesh=mesh, in_specs=in_specs, out_specs=out_specs, check_vma=False
    )
```

```python
import math

import jax
import jax.numpy as jnp
import ml_dtypes
import numpy as np
from jax import lax
from jax.experimental import pallas as pl
from jax.experimental.pallas import tpu as pltpu
from jax.sharding import PartitionSpec as P

STEPS = 16
NODES = 4
SWEEPS = 8
GX = 32
GY = 256
NZ = 64

DIFFUSION = 0.5
REACTION = 1.0


def legendre_pair(degree, point):
    previous_term, current_term = (1.0, point)
    for degree_now in range(1, degree):
        previous_term, current_term = (
            current_term,
            ((2 * degree_now + 1) * point * current_term - degree_now * previous_term)
            / (degree_now + 1),
        )
    return (current_term, previous_term)


def radau_value(count, point):
    high_term, low_term = legendre_pair(count, point)
    return high_term - low_term


def radau_points(count):
    roots_found = []
    samples = 4000
    for sample_index in range(samples):
        left_end = -1.0 + 2.0 * sample_index / samples
        right_end = -1.0 + 2.0 * (sample_index + 1) / samples
        if radau_value(count, left_end) * radau_value(count, right_end) < 0.0:
            for halving in range(200):
                middle = 0.5 * (left_end + right_end)
                if radau_value(count, left_end) * radau_value(count, middle) <= 0.0:
                    right_end = middle
                else:
                    left_end = middle
            roots_found.append(0.5 * (left_end + right_end))
    roots_found.append(1.0)
    return [(root_value + 1.0) / 2.0 for root_value in roots_found]


def collocation_matrix(node_count):
    points = radau_points(node_count)
    node_table = [[0.0] * node_count for row_number in range(node_count)]
    for column in range(node_count):
        coeffs = [1.0]
        for another in range(node_count):
            if another != column:
                spacing = points[column] - points[another]
                raised = [0.0] + coeffs
                lowered = [entry * points[another] for entry in coeffs] + [0.0]
                coeffs = [
                    (first_entry - second_entry) / spacing
                    for first_entry, second_entry in zip(raised, lowered)
                ]
        integral = [0.0] + [
            entry / (exponent_index + 1) for exponent_index, entry in enumerate(coeffs)
        ]
        for row_number in range(node_count):
            running = 0.0
            for exponent_index in range(len(integral) - 1, -1, -1):
                running = running * points[row_number] + integral[exponent_index]
            node_table[row_number][column] = running
    return node_table


def sine_matrix(count):
    index = np.arange(1, count + 1)
    return math.sqrt(2.0 / (count + 1)) * np.sin(np.pi * np.outer(index, index) / (count + 1))


def eigenvalues(count):
    return 2.0 * np.cos(np.pi * np.arange(1, count + 1) / (count + 1))


def tables():
    coll = np.array(collocation_matrix(NODES))
    sx, sy, sz = (sine_matrix(n) for n in (GX, GY, NZ))
    lam_z, lam_x, lam_y = (eigenvalues(n) for n in (NZ, GX, GY))
    kx = np.einsum("pcx,fg->cpfgx", sx.reshape(16, 2, GX), np.eye(8)).reshape(2, 128, 256)
    n = np.arange(STEPS)
    real_dft = np.zeros((8, 2, STEPS))
    for q in range(8):
        real_dft[q, 0] = np.cos(2 * np.pi * q * n / STEPS)
        real_dft[q, 1] = -np.sin(2 * np.pi * q * n / STEPS) if q else np.cos(np.pi * n)
    shifted = np.zeros_like(real_dft)
    shifted[:, :, :-1] = real_dft[:, :, 1:]
    split = real_dft.reshape(8, 2, 8, 2)
    shifted = shifted.reshape(8, 2, 8, 2)
    nodes = np.eye(NODES).reshape(NODES, 2, 2)
    last = np.zeros((NODES, 2, 2))
    last[:, 1, 1] = 1.0
    two = np.eye(2)
    form = "qrsn,mtj,zw->qrmzstnjw"
    m0 = np.zeros((128, 2, 128))
    m1 = np.zeros((128, 2, 128))
    m0[:, 0] = -np.einsum(form, split, nodes, two).reshape(128, 128)
    m0[:, 1] = np.einsum(form, split, coll.reshape(NODES, 2, 2), two).reshape(128, 128)
    m1[:, 0] = np.einsum(form, shifted, last, two).reshape(128, 128)
    m0, m1 = m0.reshape(128, 256), m1.reshape(128, 256)
    mi = np.einsum("qrsn,mtj,zw->stnjwqrmz", split, nodes, two).reshape(128, 128)
    zf = np.einsum("mn,ksz->mksnz", np.eye(4), sz.reshape(NZ, 32, 2)).reshape(256, 256)
    lam_xy = lam_x.reshape(16, 2).T[:, :, None, None] + lam_y
    lam_xy = np.broadcast_to(lam_xy, (2, 16, 8, 256)).reshape(2, 128, 256)
    lam_zy = lam_z[None, :, None] + lam_y.reshape(2, 1, 128)
    lam_x = np.broadcast_to(lam_x[:, None, None], (GX, 8, 128))
    start = np.linalg.solve(coll, np.ones(NODES))
    exact = dict(lam_xy=lam_xy, m0=m0, m1=m1, mi=mi, lam_zy=lam_zy, lam_x=lam_x)
    arrays = dict(sy=halves(sy), kx=halves(kx))
    arrays.update({k: np.asarray(v, np.float32) for k, v in exact.items()})
    kt = kx.transpose(0, 2, 1)
    arrays.update(zf=halves(zf), zt=halves(zf.T), kt=halves(kt))
    return coll, start, arrays


def halves(matrix):
    matrix = np.asarray(matrix, np.float32)
    upper = matrix.astype(ml_dtypes.bfloat16)
    lower = (matrix - upper.astype(np.float32)).astype(ml_dtypes.bfloat16)
    return np.stack([upper, lower])


COLL, START, TABLES = tables()
NAMES = tuple(TABLES)


def parts(x):
    upper = x.astype(jnp.bfloat16)
    return upper, (x - upper.astype(jnp.float32)).astype(jnp.bfloat16)


def dot3(a, b):
    one = lambda x, y: jnp.dot(x, y, preferred_element_type=jnp.float32)
    return one(a[0], b[0]) + (one(a[0], b[1]) + one(a[1], b[0]))


def horner_tables(q, params, coef, tab, lam):
    partner = (16 - q) % 16 + 8 * ((8 - q) // 8)
    own = params[2 * (q // 2)] + params[2 * (q // 2) + 1]
    mate = params[2 * (partner // 2)] + params[2 * (partner // 2) + 1]
    row = lax.broadcasted_iota(jnp.int32, (8, 128), 0)
    odd = q % 2 == 1
    own = jnp.where(odd, pltpu.roll(own, 4, 0), own)
    mate = jnp.where(odd, mate, pltpu.roll(mate, 4, 0))
    x = jnp.where(row < 4, own, mate)
    bre, bim, mre, mim, dre, dim = [x if c == 0 else pltpu.roll(x, 128 - 16 * c, 1) for c in range(6)]
    pre, pim = bre * mre - bim * mim, bre * mim + bim * mre
    scale = 6.0 * DIFFUSION - REACTION
    ere, eim = 1.0 + scale * dre, scale * dim
    mag = ere * ere + eim * eim
    gre, gim = ere / mag, -eim / mag
    are, aim = DIFFUSION * dre, DIFFUSION * dim
    rre, rim = are * gre - aim * gim, are * gim + aim * gre
    first = q == 0
    for power in range(SWEEPS):
        tre, tim = pre * gre - pim * gim, pre * gim + pim * gre
        gre, gim = gre * rre - gim * rim, gre * rim + gim * rre
        kre, kim = (jnp.sum(v[0:4], axis=0, keepdims=True) for v in (tre, tim))
        ore, oim = (jnp.sum(v[4:8], axis=0, keepdims=True) for v in (tre, tim))
        both = kre + ore
        coef[0, power : power + 1, :] = jnp.where(first, kre, both)
        coef[1, power : power + 1, :] = jnp.where(first, 0.0, kim - oim)
        coef[2, power : power + 1, :] = jnp.where(first, ore, both)

    def entry(e, carry):
        following = []
        for a, c in enumerate(carry):
            col = jnp.broadcast_to(c[:, 0:1], (8, 128))
            acc = jnp.broadcast_to(col[SWEEPS - 1 : SWEEPS], (64, 128))
            for power in range(SWEEPS - 2, -1, -1):
                acc = acc * lam + col[power : power + 1]
            tab[a, e] = acc
            following.append(pltpu.roll(c, 127, 1))
        return tuple(following)

    lax.fori_loop(0, 16, entry, (coef[0], coef[1], coef[2]))


def pack_params(node, mix, back, shifts, out):
    row = lax.broadcasted_iota(jnp.int32, (8, 128), 0)
    lane = lax.broadcasted_iota(jnp.int32, (8, 128), 1)
    kind, i, j = lane // 16, (lane // 4) % 4, lane % 4
    k, m = row // 4, row % 4
    acc = jnp.zeros((8, 128), jnp.float32)
    for c in range(2):
        for kk in range(2):
            here = k == kk
            for l in range(2):
                mine = 2 * node + l
                at_mix = here & (kind == 2 + c) & (m == mine)
                at_back = here & (kind == c) & (i == mine)
                for n in range(4):
                    acc = jnp.where(at_mix & (j == n), mix[c, kk, l, n], acc)
                    acc = jnp.where(at_back & (m == n), back[c, kk, l, n], acc)
                acc = jnp.where(here & (kind == 4 + c) & (m == mine), shifts[c, kk, l], acc)
    out[...] = acc


def kernel(u_hbm, init_hbm, alpha_hbm, mix_hbm, back_hbm, shifts_hbm, *refs):
    consts = dict(zip(NAMES, refs[: len(NAMES)]))
    refs = refs[len(NAMES) :]
    out_u, out_r = refs[:2]
    refs = refs[2:]
    held = dict(zip(NAMES, refs[: len(NAMES)]))
    refs = refs[len(NAMES) :]
    (u_ref, init_ref, su, sf, r1, sp, rp, s2, r2, s3, r3, s4, r4, halo, grid, ub, wb, wedge, whalo, before, coef, tab,
     mm, mb, sw, ow, alpha_ref, mix_ref, back_ref, shifts_ref, heard, load_sem, send_sem, recv_sem) = refs
    step, node, space = (lax.axis_index(a) for a in ("step", "node", "space"))
    me = step * 2 + node
    q, chunk, half = space // 4, (space // 2) % 2, space % 2

    load_u = pltpu.make_async_copy(u_hbm, u_ref, load_sem.at[len(NAMES)])
    load_init = pltpu.make_async_copy(init_hbm, init_ref, load_sem.at[len(NAMES) + 1])
    load_u.start()
    loads = {}
    for index, name in enumerate(NAMES):
        loads[name] = pltpu.make_async_copy(consts[name], held[name], load_sem.at[index])
    loads["sy"].start()
    loads["kx"].start()
    small = [
        pltpu.make_async_copy(src, dst, load_sem.at[len(NAMES) + 2 + i])
        for i, (src, dst) in enumerate(
            [(alpha_hbm, alpha_ref), (mix_hbm, mix_ref), (back_hbm, back_ref), (shifts_hbm, shifts_ref)])
    ]
    def get(name):
        loads[name].wait()
        return held[name]

    barrier = pltpu.get_barrier_semaphore()

    def group_id(d):
        other = (me + d) % 16
        return other, {"step": other // 2, "node": other % 2}

    def greet_group(d, _):
        pl.semaphore_signal(barrier, inc=1, device_id=group_id(d)[1])
        return 0

    def near(d):
        return {"space": (space + d) % 32}

    lax.fori_loop(1, 16, greet_group, 0)
    for d in (1, 31):
        pl.semaphore_signal(barrier, inc=1, device_id=near(d))

    def tell(turn):
        for d in (1 << turn, 32 - (1 << turn)):
            pl.semaphore_signal(heard.at[turn], inc=1, device_id=near(d))

    def hear(turn):
        pl.semaphore_wait(heard.at[turn], 2)

    load_u.wait()
    get("sy"), get("kx")
    sy = (held["sy"][0], held["sy"][1])

    def to_sines(field):
        return parts(dot3(parts(field), sy))

    def x_sines(c, rows):
        return dot3((held["kx"][0, c], held["kx"][1, c]), rows)

    rows = to_sines(u_ref[...].reshape(256, 256))
    for c in range(2):
        su[c] = x_sines(c, rows).reshape(16, 8, 256)
    load_init.start()
    for copy in small:
        copy.start()
    for name in NAMES[2:]:
        loads[name].start()
    pl.semaphore_wait(barrier, 17)
    tell(0)

    def remote(src, dst, sem, device, recv=None):
        recv = sem if recv is None else recv
        return pltpu.make_async_remote_copy(
            src_ref=src, dst_ref=dst, send_sem=send_sem.at[sem], recv_sem=recv_sem.at[recv], device_id=device
        )

    up, down = {"space": (space + 1) % 32}, {"space": (space + 31) % 32}
    HALO_UP, HALO_DOWN, PARAMS, SPACE, W_UP, W_DOWN, BEFORE = range(7)
    OTHER, FIELD, FORCE, BACK, CORR = 8, 10, 12, 14, 16
    pending = [
        remote(u_hbm.at[:, 1], halo.at[0], HALO_UP, up),
        remote(u_hbm.at[:, 0], halo.at[1], HALO_DOWN, down),
    ]
    not_first, not_last = space > 0, space < 31

    @pl.when(not_last)
    def _():
        pending[0].start()

    @pl.when(not_first)
    def _():
        pending[1].start()

    @pl.when(space == 0)
    def _():
        halo[0] = jnp.zeros((4, 32, 256), jnp.float32)

    @pl.when(space == 31)
    def _():
        halo[1] = jnp.zeros((4, 32, 256), jnp.float32)

    def to_group(src, dst, sem):
        def body(d, _):
            other, device = group_id(d)
            remote(src.at[other], dst.at[me], sem, device).start()
            return 0

        lax.fori_loop(1, 16, body, 0)
        dst[me] = src[me]

    def block_of(ref, count):
        return ref.at[pl.ds(0, count)]

    def arrived(ref, sem, count):
        part = block_of(ref, count)
        remote(part, part, sem, up).wait_recv()

    def sent(ref, sem, count):
        part = block_of(ref, count)
        remote(part, part, sem, up).wait_send()

    for c in range(2):
        to_group(su.at[c], r1.at[c, 0], FIELD + c)
    hear(0)
    tell(1)

    for copy in small:
        copy.wait()
    pack_params(node, mix_ref, back_ref, shifts_ref, sp)

    def send_params(d, _):
        remote(sp, rp.at[me], PARAMS, group_id(d)[1]).start()
        return 0

    rate = alpha_ref[0].astype(jnp.float32) * (math.log(2.0) / 16.0 / STEPS)
    col = lax.broadcasted_iota(jnp.int32, (1, 256), 1) % 128
    when = (2 * (col // 16) + (col // 4) % 2).astype(jnp.float32)
    scaled = get("m0")[...] * jnp.exp(-rate * when) + get("m1")[...] * jnp.exp(-rate * (when + 1.0))
    mm[0], mm[1] = parts(scaled)
    row = lax.broadcasted_iota(jnp.int32, (128, 128), 0)
    when = (2 * (row // 16) + (row // 4) % 2).astype(jnp.float32)
    mb[0], mb[1] = parts(get("mi")[...] * (jnp.exp(rate * when) * (1.0 / STEPS)))

    begin = [
        jnp.where(step == 0, jnp.where(node == 0, START[m], START[2 + m]), 0.0).astype(jnp.float32) for m in range(2)
    ]
    load_init.wait()
    get("lam_xy")
    hear(1)
    tell(2)

    @pl.when(not_first)
    def _():
        pending[0].wait_recv()

    @pl.when(not_last)
    def _():
        pending[1].wait_recv()

    for nm in range(4):
        for z in range(2):
            u = u_ref[nm, z]
            beside = DIFFUSION * u_ref[nm, 1 - z] + DIFFUSION * halo[z, nm]
            value = beside - (6.0 * DIFFUSION - REACTION) * u - REACTION * (u * u * u)
            if nm < 2:
                value = value + begin[nm] * init_ref[z]
            grid[nm * 2 + z] = value
    rows = to_sines(grid[...].reshape(256, 256))
    for c in range(2):
        value = x_sines(c, rows) + DIFFUSION * held["lam_xy"][c] * su[c].reshape(128, 256)
        sf[c] = value.reshape(16, 8, 256)
        to_group(sf.at[c], r1.at[c, 1], FORCE + c)
        if c == 0:
            hear(2)
            tell(3)
    lax.fori_loop(1, 16, send_params, 0)
    rp[me] = sp[...]

    for c in range(2):
        arrived(r1.at[c, 0], FIELD + c, 15)
        arrived(r1.at[c, 1], FORCE + c, 15)
        spec = dot3((mm[0], mm[1]), parts(r1[c].reshape(256, 256))).reshape(8, 2, 8, 256)
        for h in range(2):
            for part in range(2):
                s2[c, h, :, :, part * 128 : part * 128 + 128] = spec[:, part, :, h * 128 : h * 128 + 128]
        if c == 0:
            hear(3)
        for h in range(2):
            def send_spec(d, _):
                other = (q + d) % 8
                place = 4 * other + 2 * c + h
                @pl.when(place != space)
                def _():
                    remote(s2.at[c, h, other], r2.at[space], SPACE, {"space": place}).start()
                return 0

            lax.fori_loop(0, 8, send_spec, 0)
    r2[space] = s2[chunk, half, q]
    other_u = [
        remote(u_hbm.at[pl.ds(2 * i, 2)], ub.at[node, pl.ds(2 * i, 2)], OTHER + i, {"node": 1 - node}) for i in range(2)
    ]
    other_u[0].start()
    ub[node] = u_ref[...]

    arrived(rp, PARAMS, 15)
    lam = get("lam_zy")[half] + jnp.broadcast_to(get("lam_x")[2 * me + chunk][0:1], (64, 128))
    horner_tables(q, rp, coef, tab, lam)
    get("zf"), get("zt")
    arrived(r2, SPACE, 31)
    sw[...] = dot3((held["zf"][0], held["zf"][1]), parts(r2[...].reshape(256, 256))).reshape(4, 64, 256)

    def solve(z, _):
        at = pl.ds(pl.multiple_of(z * 8, 8), 8)
        re_in = [sw[i, at, 0:128] for i in range(4)]
        im_in = [sw[i, at, 128:256] for i in range(4)]
        for i in range(4):
            re = im = None
            for j in range(4):
                a, e, d = (tab[c, 4 * i + j, at, :] for c in range(3))
                tre, tim = a * re_in[j] - e * im_in[j], e * re_in[j] + d * im_in[j]
                re, im = (tre, tim) if re is None else (re + tre, im + tim)
            ow[i, at, 0:128] = re
            ow[i, at, 128:256] = im
        return 0

    lax.fori_loop(0, 8, solve, 0)
    value = dot3((held["zt"][0], held["zt"][1]), parts(ow[...].reshape(256, 256))).reshape(32, 8, 256)
    for part in range(2):
        s3[:, part] = value[:, :, part * 128 : part * 128 + 128]

    def send_back(d, _):
        other = (space + d) % 32
        remote(s3.at[other], r3.at[chunk, half, q], BACK, {"space": other}, BACK + chunk).start()
        return 0

    lax.fori_loop(1, 32, send_back, 0)
    other_u[1].start()
    r3[chunk, half, q] = s3[space]
    get("kt")
    for c in range(2):
        for here in range(2):
            @pl.when((chunk == c) if here else (chunk != c))
            def _():
                part = block_of(s3, 16 - here)
                remote(part, part, BACK, up, BACK + c).wait_recv()
        for h in range(2):
            value = dot3((mb[0], mb[1]), parts(r3[c, h].reshape(128, 128)))
            s4[c, :, :, :, h * 128 : h * 128 + 128] = value.reshape(8, 2, 8, 128)

        def send_corr(d, _):
            other, device = group_id(d)
            remote(s4.at[c, other // 2], r4.at[c, :, me], CORR + c, device).start()
            return 0

        lax.fori_loop(1, 16, send_corr, 0)
        r4[c, :, me] = s4[c, step]
    for copy in other_u:
        copy.wait_recv()
    for c in range(2):
        whole = r4.at[c, :, pl.ds(0, 15)]
        remote(whole, whole, CORR + c, up).wait_recv()
        for g in range(2):
            rows = to_sines(r4[c, g].reshape(128, 256))
            d = dot3((held["kt"][0, c], held["kt"][1, c]), rows)
            ub[g] = ub[g] + d.reshape(4, 2, 32, 256)
    out_u[...] = ub[node] - u_ref[...]

    weight = [
        [jnp.where(node == 0, COLL[m][j], COLL[2 + m][j]).astype(jnp.float32) for j in range(4)] for m in range(2)
    ]

    def nodes_at(n, z):
        return [ub[j // 2, 2 * n + j % 2, z] for j in range(4)]

    seam_up, seam_down = (space % 16) // 15, (space + 15) % 16 // 15
    above = {"space": (space + 1) % 32, "node": (node + seam_up) % 2}
    below = {"space": (space + 31) % 32, "node": (node + seam_down) % 2}
    target = [(node + seam_down) % 2, (node + seam_up) % 2]
    for n in range(2):
        for z in range(2):
            u = nodes_at(n, z)
            for m in range(2):
                wb[2 * n + m, z] = sum(weight[m][j] * u[j] for j in range(4))
                rows = [jnp.where(target[z] == 0, COLL[m][j], COLL[2 + m][j]).astype(jnp.float32) for j in range(4)]
                wedge[z, 2 * n + m] = sum(rows[j] * u[j] for j in range(4))
    last = [
        remote(wedge.at[1], whalo.at[0], W_UP, above),
        remote(wedge.at[0], whalo.at[1], W_DOWN, below),
        remote(ub.at[1, 3], before, BEFORE, {"step": (step + 1) % 8}),
    ]
    for copy in last:
        copy.start()
    x = lax.broadcasted_iota(jnp.int32, (32, 256), 0)
    y = lax.broadcasted_iota(jnp.int32, (32, 256), 1)
    for n in range(2):
        for z in range(2):
            cubes = [v * v * v for v in nodes_at(n, z)]
            for m in range(2):
                w = wb[2 * n + m, z]
                beside = (
                    wb[2 * n + m, 1 - z]
                    + jnp.where(x == 0, 0.0, pltpu.roll(w, 1, 0))
                    + jnp.where(x == 31, 0.0, pltpu.roll(w, 31, 0))
                    + jnp.where(y == 0, 0.0, pltpu.roll(w, 1, 1))
                    + jnp.where(y == 255, 0.0, pltpu.roll(w, 255, 1))
                )
                value = DIFFUSION * beside - (6.0 * DIFFUSION - REACTION) * w
                value = value - REACTION * sum(weight[m][j] * cubes[j] for j in range(4))
                if n == 1:
                    value = value + ub[1, 1, z]
                out_r[2 * n + m, z] = value
    for copy in last:
        copy.wait_recv()
    low = jnp.where(space == 0, 0.0, DIFFUSION)
    high = jnp.where(space == 31, 0.0, DIFFUSION)
    for z in range(2):
        opening = jnp.where(step == 0, init_ref[z], before[z])
        for nm in range(4):
            edge = (low if z == 0 else high) * whalo[z, nm]
            out_r[nm, z] = out_r[nm, z] + (edge + opening if nm < 2 else edge)

    @pl.when(not_last)
    def _():
        pending[0].wait_send()

    @pl.when(not_first)
    def _():
        pending[1].wait_send()

    for copy in last + other_u:
        copy.wait_send()
    for c in range(2):
        sent(su.at[c], FIELD + c, 15)
        sent(sf.at[c], FORCE + c, 15)
        whole = r4.at[c, :, pl.ds(0, 15)]
        remote(whole, whole, CORR + c, up).wait_send()
    sent(rp, PARAMS, 15)
    sent(r2, SPACE, 31)
    sent(s3, BACK, 31)


def on_device(iterate, initial_value, alpha_power, node_mix, node_back, shifts):
    consts = [jnp.asarray(TABLES[name]) for name in NAMES]
    f32 = jnp.float32
    vmem = lambda *shape: pltpu.VMEM(shape, f32)
    block = jax.ShapeDtypeStruct((4, 2, 32, 256), f32)
    in_vmem, in_any = (pl.BlockSpec(memory_space=m) for m in (pltpu.VMEM, pltpu.HBM))
    correction, rest = pl.pallas_call(
        kernel,
        out_shape=(block, block),
        in_specs=[in_any] * (6 + len(NAMES)),
        out_specs=(in_vmem, in_vmem),
        scratch_shapes=[pltpu.VMEM(TABLES[name].shape, TABLES[name].dtype) for name in NAMES]
        + [vmem(4, 2, 32, 256), vmem(2, 32, 256)]
        + [vmem(2, 16, 8, 256)] * 2
        + [vmem(2, 2, 16, 8, 256)]
        + [vmem(8, 128), vmem(16, 8, 128)]
        + [vmem(2, 2, 8, 8, 256), vmem(32, 8, 256)]
        + [vmem(32, 2, 8, 128), vmem(2, 2, 8, 2, 8, 128)]
        + [vmem(2, 8, 2, 8, 256), vmem(2, 2, 16, 8, 256)]
        + [vmem(2, 4, 32, 256), vmem(8, 32, 256)]
        + [vmem(2, 4, 2, 32, 256), vmem(4, 2, 32, 256)]
        + [vmem(2, 4, 32, 256)] * 2 + [vmem(2, 32, 256)]
        + [vmem(3, 8, 128), vmem(3, 16, 64, 128)]
        + [pltpu.VMEM((2, 128, 256), jnp.bfloat16), pltpu.VMEM((2, 128, 128), jnp.bfloat16)]
        + [vmem(4, 64, 256)] * 2
        + [pltpu.SMEM((1,), jnp.int32), pltpu.SMEM((2, 2, 2, 4), f32), pltpu.SMEM((2, 2, 2, 4), f32), pltpu.SMEM((2, 2, 2), f32)]
        + [pltpu.SemaphoreType.REGULAR((4,))]
        + [pltpu.SemaphoreType.DMA((len(NAMES) + 6,)), pltpu.SemaphoreType.DMA((18,)), pltpu.SemaphoreType.DMA((18,))],
        compiler_params=pltpu.CompilerParams(
            collective_id=0, has_side_effects=True, vmem_limit_bytes=63 * 1024 * 1024
        ),
    )(iterate.reshape(4, 2, 32, 256), initial_value, alpha_power, node_mix, node_back, shifts, *consts)
    updated = iterate + correction.reshape(iterate.shape)
    return updated, rest.reshape(iterate.shape) - updated


def solution(mesh):
    in_specs = (
        P("step", "node", "space", None, None),
        P("space", None, None),
        P(),
        P(None, "step", "node", None),
        P(None, "step", "node", None),
        P(None, "step", "node"),
    )
    out_specs = (P("step", "node", "space", None, None), P("step", "node", "space", None, None))
    return jax.shard_map(
        on_device, mesh=mesh, in_specs=in_specs, out_specs=out_specs, check_vma=False
    )
```

```python
import math

import jax
import jax.numpy as jnp
import ml_dtypes
import numpy as np
from jax import lax
from jax.experimental import pallas as pl
from jax.experimental.pallas import tpu as pltpu
from jax.sharding import PartitionSpec as P

STEPS = 16
NODES = 4
SWEEPS = 8
GX = 32
GY = 256
NZ = 64

DIFFUSION = 0.5
REACTION = 1.0


def legendre_pair(degree, point):
    previous_term, current_term = (1.0, point)
    for degree_now in range(1, degree):
        previous_term, current_term = (
            current_term,
            ((2 * degree_now + 1) * point * current_term - degree_now * previous_term)
            / (degree_now + 1),
        )
    return (current_term, previous_term)


def radau_value(count, point):
    high_term, low_term = legendre_pair(count, point)
    return high_term - low_term


def radau_points(count):
    roots_found = []
    samples = 4000
    for sample_index in range(samples):
        left_end = -1.0 + 2.0 * sample_index / samples
        right_end = -1.0 + 2.0 * (sample_index + 1) / samples
        if radau_value(count, left_end) * radau_value(count, right_end) < 0.0:
            for halving in range(200):
                middle = 0.5 * (left_end + right_end)
                if radau_value(count, left_end) * radau_value(count, middle) <= 0.0:
                    right_end = middle
                else:
                    left_end = middle
            roots_found.append(0.5 * (left_end + right_end))
    roots_found.append(1.0)
    return [(root_value + 1.0) / 2.0 for root_value in roots_found]


def collocation_matrix(node_count):
    points = radau_points(node_count)
    node_table = [[0.0] * node_count for row_number in range(node_count)]
    for column in range(node_count):
        coeffs = [1.0]
        for another in range(node_count):
            if another != column:
                spacing = points[column] - points[another]
                raised = [0.0] + coeffs
                lowered = [entry * points[another] for entry in coeffs] + [0.0]
                coeffs = [
                    (first_entry - second_entry) / spacing
                    for first_entry, second_entry in zip(raised, lowered)
                ]
        integral = [0.0] + [
            entry / (exponent_index + 1) for exponent_index, entry in enumerate(coeffs)
        ]
        for row_number in range(node_count):
            running = 0.0
            for exponent_index in range(len(integral) - 1, -1, -1):
                running = running * points[row_number] + integral[exponent_index]
            node_table[row_number][column] = running
    return node_table


def sine_matrix(count):
    index = np.arange(1, count + 1)
    return math.sqrt(2.0 / (count + 1)) * np.sin(np.pi * np.outer(index, index) / (count + 1))


def eigenvalues(count):
    return 2.0 * np.cos(np.pi * np.arange(1, count + 1) / (count + 1))


def tables():
    coll = np.array(collocation_matrix(NODES))
    sx, sy, sz = (sine_matrix(n) for n in (GX, GY, NZ))
    lam_z, lam_x, lam_y = (eigenvalues(n) for n in (NZ, GX, GY))
    kx = np.einsum("pcx,fg->cpfgx", sx.reshape(16, 2, GX), np.eye(8)).reshape(2, 128, 256)
    n = np.arange(STEPS)
    real_dft = np.zeros((8, 2, STEPS))
    for q in range(8):
        real_dft[q, 0] = np.cos(2 * np.pi * q * n / STEPS)
        real_dft[q, 1] = -np.sin(2 * np.pi * q * n / STEPS) if q else np.cos(np.pi * n)
    shifted = np.zeros_like(real_dft)
    shifted[:, :, :-1] = real_dft[:, :, 1:]
    split = real_dft.reshape(8, 2, 8, 2)
    shifted = shifted.reshape(8, 2, 8, 2)
    nodes = np.eye(NODES).reshape(NODES, 2, 2)
    last = np.zeros((NODES, 2, 2))
    last[:, 1, 1] = 1.0
    two = np.eye(2)
    form = "qrsn,mtj,zw->qrmzstnjw"
    m0 = np.zeros((128, 2, 128))
    m1 = np.zeros((128, 2, 128))
    m0[:, 0] = -np.einsum(form, split, nodes, two).reshape(128, 128)
    m0[:, 1] = np.einsum(form, split, coll.reshape(NODES, 2, 2), two).reshape(128, 128)
    m1[:, 0] = np.einsum(form, shifted, last, two).reshape(128, 128)
    m0, m1 = m0.reshape(128, 256), m1.reshape(128, 256)
    mi = np.einsum("qrsn,mtj,zw->stnjwqrmz", split, nodes, two).reshape(128, 128)
    zf = np.einsum("mn,ksz->mksnz", np.eye(4), sz.reshape(NZ, 32, 2)).reshape(256, 256)
    lam_xy = lam_x.reshape(16, 2).T[:, :, None, None] + lam_y
    lam_xy = np.broadcast_to(lam_xy, (2, 16, 8, 256)).reshape(2, 128, 256)
    lam_zy = lam_z[None, :, None] + lam_y.reshape(2, 1, 128)
    lam_x = np.broadcast_to(lam_x[:, None, None], (GX, 8, 128))
    start = np.linalg.solve(coll, np.ones(NODES))
    exact = dict(lam_xy=lam_xy, m0=m0, m1=m1, mi=mi, lam_zy=lam_zy, lam_x=lam_x)
    arrays = dict(sy=halves(sy), kx=halves(kx))
    arrays.update({k: np.asarray(v, np.float32) for k, v in exact.items()})
    kt = kx.transpose(0, 2, 1)
    arrays.update(zf=halves(zf), zt=halves(zf.T), kt=halves(kt))
    return coll, start, arrays


def halves(matrix):
    matrix = np.asarray(matrix, np.float32)
    upper = matrix.astype(ml_dtypes.bfloat16)
    lower = (matrix - upper.astype(np.float32)).astype(ml_dtypes.bfloat16)
    return np.stack([upper, lower])


COLL, START, TABLES = tables()
NAMES = tuple(TABLES)


def parts(x):
    upper = x.astype(jnp.bfloat16)
    return upper, (x - upper.astype(jnp.float32)).astype(jnp.bfloat16)


def dot3(a, b):
    one = lambda x, y: jnp.dot(x, y, preferred_element_type=jnp.float32)
    return one(a[0], b[0]) + (one(a[0], b[1]) + one(a[1], b[0]))


def horner_tables(q, params, coef, tab, lam):
    partner = (16 - q) % 16 + 8 * ((8 - q) // 8)
    own = params[2 * (q // 2)] + params[2 * (q // 2) + 1]
    mate = params[2 * (partner // 2)] + params[2 * (partner // 2) + 1]
    row = lax.broadcasted_iota(jnp.int32, (8, 128), 0)
    odd = q % 2 == 1
    own = jnp.where(odd, pltpu.roll(own, 4, 0), own)
    mate = jnp.where(odd, mate, pltpu.roll(mate, 4, 0))
    x = jnp.where(row < 4, own, mate)
    bre, bim, mre, mim, dre, dim = [x if c == 0 else pltpu.roll(x, 128 - 16 * c, 1) for c in range(6)]
    pre, pim = bre * mre - bim * mim, bre * mim + bim * mre
    scale = 6.0 * DIFFUSION - REACTION
    ere, eim = 1.0 + scale * dre, scale * dim
    mag = ere * ere + eim * eim
    gre, gim = ere / mag, -eim / mag
    are, aim = DIFFUSION * dre, DIFFUSION * dim
    rre, rim = are * gre - aim * gim, are * gim + aim * gre
    first = q == 0
    for power in range(SWEEPS):
        tre, tim = pre * gre - pim * gim, pre * gim + pim * gre
        gre, gim = gre * rre - gim * rim, gre * rim + gim * rre
        kre, kim = (jnp.sum(v[0:4], axis=0, keepdims=True) for v in (tre, tim))
        ore, oim = (jnp.sum(v[4:8], axis=0, keepdims=True) for v in (tre, tim))
        both = kre + ore
        coef[0, power : power + 1, :] = jnp.where(first, kre, both)
        coef[1, power : power + 1, :] = jnp.where(first, 0.0, kim - oim)
        coef[2, power : power + 1, :] = jnp.where(first, ore, both)

    def entry(e, carry):
        following = []
        for a, c in enumerate(carry):
            col = jnp.broadcast_to(c[:, 0:1], (8, 128))
            acc = jnp.broadcast_to(col[SWEEPS - 1 : SWEEPS], (64, 128))
            for power in range(SWEEPS - 2, -1, -1):
                acc = acc * lam + col[power : power + 1]
            tab[a, e] = acc
            following.append(pltpu.roll(c, 127, 1))
        return tuple(following)

    lax.fori_loop(0, 16, entry, (coef[0], coef[1], coef[2]))


def pack_params(node, mix, back, shifts, out):
    row = lax.broadcasted_iota(jnp.int32, (8, 128), 0)
    lane = lax.broadcasted_iota(jnp.int32, (8, 128), 1)
    kind, i, j = lane // 16, (lane // 4) % 4, lane % 4
    k, m = row // 4, row % 4
    acc = jnp.zeros((8, 128), jnp.float32)
    for c in range(2):
        for kk in range(2):
            here = k == kk
            for l in range(2):
                mine = 2 * node + l
                at_mix = here & (kind == 2 + c) & (m == mine)
                at_back = here & (kind == c) & (i == mine)
                for n in range(4):
                    acc = jnp.where(at_mix & (j == n), mix[c, kk, l, n], acc)
                    acc = jnp.where(at_back & (m == n), back[c, kk, l, n], acc)
                acc = jnp.where(here & (kind == 4 + c) & (m == mine), shifts[c, kk, l], acc)
    out[...] = acc


def kernel(u_hbm, init_hbm, alpha_hbm, mix_hbm, back_hbm, shifts_hbm, *refs):
    consts = dict(zip(NAMES, refs[: len(NAMES)]))
    refs = refs[len(NAMES) :]
    out_u, out_r = refs[:2]
    refs = refs[2:]
    held = dict(zip(NAMES, refs[: len(NAMES)]))
    refs = refs[len(NAMES) :]
    (u_ref, init_ref, su, sf, r1, sp, rp, s2, r2, s3, r3, s4, r4, halo, grid, ub, wb, wedge, whalo, before, coef, tab,
     mm, mb, sw, ow, alpha_ref, mix_ref, back_ref, shifts_ref, heard, load_sem, send_sem, recv_sem) = refs
    step, node, space = (lax.axis_index(a) for a in ("step", "node", "space"))
    me = step * 2 + node
    q, half, chunk = (space % 16) // 2, space % 2, (space // 16 + space) % 2

    load_u = pltpu.make_async_copy(u_hbm, u_ref, load_sem.at[len(NAMES)])
    load_init = pltpu.make_async_copy(init_hbm, init_ref, load_sem.at[len(NAMES) + 1])
    load_u.start()
    loads = {}
    for index, name in enumerate(NAMES):
        loads[name] = pltpu.make_async_copy(consts[name], held[name], load_sem.at[index])
    loads["sy"].start()
    loads["kx"].start()
    small = [
        pltpu.make_async_copy(src, dst, load_sem.at[len(NAMES) + 2 + i])
        for i, (src, dst) in enumerate(
            [(alpha_hbm, alpha_ref), (mix_hbm, mix_ref), (back_hbm, back_ref), (shifts_hbm, shifts_ref)])
    ]
    def get(name):
        loads[name].wait()
        return held[name]

    barrier = pltpu.get_barrier_semaphore()

    def group_id(d):
        other = (me + d) % 16
        return other, {"step": other // 2, "node": other % 2}

    def greet_group(d, _):
        pl.semaphore_signal(barrier, inc=1, device_id=group_id(d)[1])
        return 0

    def near(d):
        return {"space": (space + d) % 32}

    lax.fori_loop(1, 16, greet_group, 0)
    for d in (1, 31):
        pl.semaphore_signal(barrier, inc=1, device_id=near(d))

    def tell(turn):
        for d in (1 << turn, 32 - (1 << turn)):
            pl.semaphore_signal(heard.at[turn], inc=1, device_id=near(d))

    def hear(turn):
        pl.semaphore_wait(heard.at[turn], 2)

    load_u.wait()
    get("sy"), get("kx")
    sy = (held["sy"][0], held["sy"][1])

    def to_sines(field):
        return parts(dot3(parts(field), sy))

    def x_sines(c, rows):
        return dot3((held["kx"][0, c], held["kx"][1, c]), rows)

    rows = to_sines(u_ref[...].reshape(256, 256))
    for c in range(2):
        su[c] = x_sines(c, rows).reshape(16, 8, 256)
    load_init.start()
    for copy in small:
        copy.start()
    for name in NAMES[2:]:
        loads[name].start()
    pl.semaphore_wait(barrier, 17)
    tell(0)

    def remote(src, dst, sem, device, recv=None):
        recv = sem if recv is None else recv
        return pltpu.make_async_remote_copy(
            src_ref=src, dst_ref=dst, send_sem=send_sem.at[sem], recv_sem=recv_sem.at[recv], device_id=device
        )

    up, down = {"space": (space + 1) % 32}, {"space": (space + 31) % 32}
    HALO_UP, HALO_DOWN, PARAMS, SPACE, W_UP, W_DOWN, BEFORE = range(7)
    OTHER, FIELD, FORCE, BACK, CORR = 8, 10, 12, 14, 16
    pending = [
        remote(u_hbm.at[:, 1], halo.at[0], HALO_UP, up),
        remote(u_hbm.at[:, 0], halo.at[1], HALO_DOWN, down),
    ]
    not_first, not_last = space > 0, space < 31

    @pl.when(not_last)
    def _():
        pending[0].start()

    @pl.when(not_first)
    def _():
        pending[1].start()

    @pl.when(space == 0)
    def _():
        halo[0] = jnp.zeros((4, 32, 256), jnp.float32)

    @pl.when(space == 31)
    def _():
        halo[1] = jnp.zeros((4, 32, 256), jnp.float32)

    def to_group(src, dst, sem):
        def body(d, _):
            other, device = group_id(d)
            remote(src.at[other], dst.at[me], sem, device).start()
            return 0

        lax.fori_loop(1, 16, body, 0)
        dst[me] = src[me]

    def block_of(ref, count):
        return ref.at[pl.ds(0, count)]

    def arrived(ref, sem, count):
        part = block_of(ref, count)
        remote(part, part, sem, up).wait_recv()

    def sent(ref, sem, count):
        part = block_of(ref, count)
        remote(part, part, sem, up).wait_send()

    for c in range(2):
        to_group(su.at[c], r1.at[c, 0], FIELD + c)
    hear(0)
    tell(1)

    for copy in small:
        copy.wait()
    pack_params(node, mix_ref, back_ref, shifts_ref, sp)

    def send_params(d, _):
        remote(sp, rp.at[me], PARAMS, group_id(d)[1]).start()
        return 0

    rate = alpha_ref[0].astype(jnp.float32) * (math.log(2.0) / 16.0 / STEPS)
    col = lax.broadcasted_iota(jnp.int32, (1, 256), 1) % 128
    when = (2 * (col // 16) + (col // 4) % 2).astype(jnp.float32)
    scaled = get("m0")[...] * jnp.exp(-rate * when) + get("m1")[...] * jnp.exp(-rate * (when + 1.0))
    mm[0], mm[1] = parts(scaled)
    row = lax.broadcasted_iota(jnp.int32, (128, 128), 0)
    when = (2 * (row // 16) + (row // 4) % 2).astype(jnp.float32)
    mb[0], mb[1] = parts(get("mi")[...] * (jnp.exp(rate * when) * (1.0 / STEPS)))

    lax.fori_loop(1, 16, send_params, 0)
    rp[me] = sp[...]

    begin = [
        jnp.where(step == 0, jnp.where(node == 0, START[m], START[2 + m]), 0.0).astype(jnp.float32) for m in range(2)
    ]
    load_init.wait()
    get("lam_xy")
    hear(1)
    tell(2)

    @pl.when(not_first)
    def _():
        pending[0].wait_recv()

    @pl.when(not_last)
    def _():
        pending[1].wait_recv()

    for nm in range(4):
        for z in range(2):
            u = u_ref[nm, z]
            beside = DIFFUSION * u_ref[nm, 1 - z] + DIFFUSION * halo[z, nm]
            value = beside - (6.0 * DIFFUSION - REACTION) * u - REACTION * (u * u * u)
            if nm < 2:
                value = value + begin[nm] * init_ref[z]
            grid[nm * 2 + z] = value
    rows = to_sines(grid[...].reshape(256, 256))
    for c in range(2):
        value = x_sines(c, rows) + DIFFUSION * held["lam_xy"][c] * su[c].reshape(128, 256)
        sf[c] = value.reshape(16, 8, 256)
        to_group(sf.at[c], r1.at[c, 1], FORCE + c)
        if c == 0:
            hear(2)
            tell(3)

    for c in range(2):
        arrived(r1.at[c, 0], FIELD + c, 15)
        arrived(r1.at[c, 1], FORCE + c, 15)
        spec = dot3((mm[0], mm[1]), parts(r1[c].reshape(256, 256))).reshape(8, 2, 8, 256)
        for h in range(2):
            for part in range(2):
                s2[c, h, :, :, part * 128 : part * 128 + 128] = spec[:, part, :, h * 128 : h * 128 + 128]
        if c == 0:
            hear(3)
        for h in range(2):
            def send_spec(d, _):
                other = (q + d) % 8
                place = (h + c) % 2 * 16 + 2 * other + h
                @pl.when(place != space)
                def _():
                    remote(s2.at[c, h, other], r2.at[space], SPACE, {"space": place}).start()
                return 0

            lax.fori_loop(0, 8, send_spec, 0)
    r2[space] = s2[chunk, half, q]
    other_u = [
        remote(u_hbm.at[pl.ds(2 * i, 2)], ub.at[node, pl.ds(2 * i, 2)], OTHER + i, {"node": 1 - node}) for i in range(2)
    ]
    ub[node] = u_ref[...]

    arrived(rp, PARAMS, 15)
    lam = get("lam_zy")[half] + jnp.broadcast_to(get("lam_x")[2 * me + chunk][0:1], (64, 128))
    horner_tables(q, rp, coef, tab, lam)
    get("zf"), get("zt")
    other_u[0].start()
    other_u[1].start()
    arrived(r2, SPACE, 31)
    sw[...] = dot3((held["zf"][0], held["zf"][1]), parts(r2[...].reshape(256, 256))).reshape(4, 64, 256)

    def solve(z, _):
        at = pl.ds(pl.multiple_of(z * 8, 8), 8)
        re_in = [sw[i, at, 0:128] for i in range(4)]
        im_in = [sw[i, at, 128:256] for i in range(4)]
        for i in range(4):
            re = im = None
            for j in range(4):
                a, e, d = (tab[c, 4 * i + j, at, :] for c in range(3))
                tre, tim = a * re_in[j] - e * im_in[j], e * re_in[j] + d * im_in[j]
                re, im = (tre, tim) if re is None else (re + tre, im + tim)
            ow[i, at, 0:128] = re
            ow[i, at, 128:256] = im
        return 0

    lax.fori_loop(0, 8, solve, 0)
    value = dot3((held["zt"][0], held["zt"][1]), parts(ow[...].reshape(256, 256))).reshape(32, 8, 256)
    for part in range(2):
        s3[:, part] = value[:, :, part * 128 : part * 128 + 128]

    def send_back(d, _):
        other = (space + d) % 32
        remote(s3.at[other], r3.at[chunk, half, q], BACK, {"space": other}, BACK + chunk).start()
        return 0

    lax.fori_loop(1, 32, send_back, 0)
    r3[chunk, half, q] = s3[space]
    get("kt")
    for c in range(2):
        for here in range(2):
            @pl.when((chunk == c) if here else (chunk != c))
            def _():
                part = block_of(s3, 16 - here)
                remote(part, part, BACK, up, BACK + c).wait_recv()
        for h in range(2):
            value = dot3((mb[0], mb[1]), parts(r3[c, h].reshape(128, 128)))
            s4[c, :, :, :, h * 128 : h * 128 + 128] = value.reshape(8, 2, 8, 128)

        def send_corr(d, _):
            other, device = group_id(d)
            remote(s4.at[c, other // 2], r4.at[c, :, me], CORR + c, device).start()
            return 0

        lax.fori_loop(1, 16, send_corr, 0)
        r4[c, :, me] = s4[c, step]
    for copy in other_u:
        copy.wait_recv()
    for c in range(2):
        whole = r4.at[c, :, pl.ds(0, 15)]
        remote(whole, whole, CORR + c, up).wait_recv()
        for g in range(2):
            rows = to_sines(r4[c, g].reshape(128, 256))
            d = dot3((held["kt"][0, c], held["kt"][1, c]), rows)
            ub[g] = ub[g] + d.reshape(4, 2, 32, 256)
    out_u[...] = ub[node] - u_ref[...]

    weight = [
        [jnp.where(node == 0, COLL[m][j], COLL[2 + m][j]).astype(jnp.float32) for j in range(4)] for m in range(2)
    ]

    def nodes_at(n, z):
        return [ub[j // 2, 2 * n + j % 2, z] for j in range(4)]

    seam_up, seam_down = (space % 16) // 15, (space + 15) % 16 // 15
    above = {"space": (space + 1) % 32, "node": (node + seam_up) % 2}
    below = {"space": (space + 31) % 32, "node": (node + seam_down) % 2}
    target = [(node + seam_down) % 2, (node + seam_up) % 2]
    for n in range(2):
        for z in range(2):
            u = nodes_at(n, z)
            for m in range(2):
                wb[2 * n + m, z] = sum(weight[m][j] * u[j] for j in range(4))
                rows = [jnp.where(target[z] == 0, COLL[m][j], COLL[2 + m][j]).astype(jnp.float32) for j in range(4)]
                wedge[z, 2 * n + m] = sum(rows[j] * u[j] for j in range(4))
    last = [
        remote(wedge.at[1], whalo.at[0], W_UP, above),
        remote(wedge.at[0], whalo.at[1], W_DOWN, below),
        remote(ub.at[1, 3], before, BEFORE, {"step": (step + 1) % 8}),
    ]
    for copy in last:
        copy.start()
    x = lax.broadcasted_iota(jnp.int32, (32, 256), 0)
    y = lax.broadcasted_iota(jnp.int32, (32, 256), 1)
    for n in range(2):
        for z in range(2):
            cubes = [v * v * v for v in nodes_at(n, z)]
            for m in range(2):
                w = wb[2 * n + m, z]
                beside = (
                    wb[2 * n + m, 1 - z]
                    + jnp.where(x == 0, 0.0, pltpu.roll(w, 1, 0))
                    + jnp.where(x == 31, 0.0, pltpu.roll(w, 31, 0))
                    + jnp.where(y == 0, 0.0, pltpu.roll(w, 1, 1))
                    + jnp.where(y == 255, 0.0, pltpu.roll(w, 255, 1))
                )
                value = DIFFUSION * beside - (6.0 * DIFFUSION - REACTION) * w
                value = value - REACTION * sum(weight[m][j] * cubes[j] for j in range(4))
                if n == 1:
                    value = value + ub[1, 1, z]
                out_r[2 * n + m, z] = value
    for copy in last:
        copy.wait_recv()
    low = jnp.where(space == 0, 0.0, DIFFUSION)
    high = jnp.where(space == 31, 0.0, DIFFUSION)
    for z in range(2):
        opening = jnp.where(step == 0, init_ref[z], before[z])
        for nm in range(4):
            edge = (low if z == 0 else high) * whalo[z, nm]
            out_r[nm, z] = out_r[nm, z] + (edge + opening if nm < 2 else edge)

    @pl.when(not_last)
    def _():
        pending[0].wait_send()

    @pl.when(not_first)
    def _():
        pending[1].wait_send()

    for copy in last + other_u:
        copy.wait_send()
    for c in range(2):
        sent(su.at[c], FIELD + c, 15)
        sent(sf.at[c], FORCE + c, 15)
        whole = r4.at[c, :, pl.ds(0, 15)]
        remote(whole, whole, CORR + c, up).wait_send()
    sent(rp, PARAMS, 15)
    sent(r2, SPACE, 31)
    sent(s3, BACK, 31)


def on_device(iterate, initial_value, alpha_power, node_mix, node_back, shifts):
    consts = [jnp.asarray(TABLES[name]) for name in NAMES]
    f32 = jnp.float32
    vmem = lambda *shape: pltpu.VMEM(shape, f32)
    block = jax.ShapeDtypeStruct((4, 2, 32, 256), f32)
    in_vmem, in_any = (pl.BlockSpec(memory_space=m) for m in (pltpu.VMEM, pltpu.HBM))
    correction, rest = pl.pallas_call(
        kernel,
        out_shape=(block, block),
        in_specs=[in_any] * (6 + len(NAMES)),
        out_specs=(in_vmem, in_vmem),
        scratch_shapes=[pltpu.VMEM(TABLES[name].shape, TABLES[name].dtype) for name in NAMES]
        + [vmem(4, 2, 32, 256), vmem(2, 32, 256)]
        + [vmem(2, 16, 8, 256)] * 2
        + [vmem(2, 2, 16, 8, 256)]
        + [vmem(8, 128), vmem(16, 8, 128)]
        + [vmem(2, 2, 8, 8, 256), vmem(32, 8, 256)]
        + [vmem(32, 2, 8, 128), vmem(2, 2, 8, 2, 8, 128)]
        + [vmem(2, 8, 2, 8, 256), vmem(2, 2, 16, 8, 256)]
        + [vmem(2, 4, 32, 256), vmem(8, 32, 256)]
        + [vmem(2, 4, 2, 32, 256), vmem(4, 2, 32, 256)]
        + [vmem(2, 4, 32, 256)] * 2 + [vmem(2, 32, 256)]
        + [vmem(3, 8, 128), vmem(3, 16, 64, 128)]
        + [pltpu.VMEM((2, 128, 256), jnp.bfloat16), pltpu.VMEM((2, 128, 128), jnp.bfloat16)]
        + [vmem(4, 64, 256)] * 2
        + [pltpu.SMEM((1,), jnp.int32), pltpu.SMEM((2, 2, 2, 4), f32), pltpu.SMEM((2, 2, 2, 4), f32), pltpu.SMEM((2, 2, 2), f32)]
        + [pltpu.SemaphoreType.REGULAR((4,))]
        + [pltpu.SemaphoreType.DMA((len(NAMES) + 6,)), pltpu.SemaphoreType.DMA((18,)), pltpu.SemaphoreType.DMA((18,))],
        compiler_params=pltpu.CompilerParams(
            collective_id=0, has_side_effects=True, vmem_limit_bytes=63 * 1024 * 1024
        ),
    )(iterate.reshape(4, 2, 32, 256), initial_value, alpha_power, node_mix, node_back, shifts, *consts)
    updated = iterate + correction.reshape(iterate.shape)
    return updated, rest.reshape(iterate.shape) - updated


def solution(mesh):
    in_specs = (
        P("step", "node", "space", None, None),
        P("space", None, None),
        P(),
        P(None, "step", "node", None),
        P(None, "step", "node", None),
        P(None, "step", "node"),
    )
    out_specs = (P("step", "node", "space", None, None), P("step", "node", "space", None, None))
    return jax.shard_map(
        on_device, mesh=mesh, in_specs=in_specs, out_specs=out_specs, check_vma=False
    )
```

```python
import math

import jax
import jax.numpy as jnp
import ml_dtypes
import numpy as np
from jax import lax
from jax.experimental import pallas as pl
from jax.experimental.pallas import tpu as pltpu
from jax.sharding import PartitionSpec as P

STEPS = 16
NODES = 4
SWEEPS = 8
GX = 32
GY = 256
NZ = 64

DIFFUSION = 0.5
REACTION = 1.0


def legendre_pair(degree, point):
    previous_term, current_term = (1.0, point)
    for degree_now in range(1, degree):
        previous_term, current_term = (
            current_term,
            ((2 * degree_now + 1) * point * current_term - degree_now * previous_term)
            / (degree_now + 1),
        )
    return (current_term, previous_term)


def radau_value(count, point):
    high_term, low_term = legendre_pair(count, point)
    return high_term - low_term


def radau_points(count):
    roots_found = []
    samples = 4000
    for sample_index in range(samples):
        left_end = -1.0 + 2.0 * sample_index / samples
        right_end = -1.0 + 2.0 * (sample_index + 1) / samples
        if radau_value(count, left_end) * radau_value(count, right_end) < 0.0:
            for halving in range(200):
                middle = 0.5 * (left_end + right_end)
                if radau_value(count, left_end) * radau_value(count, middle) <= 0.0:
                    right_end = middle
                else:
                    left_end = middle
            roots_found.append(0.5 * (left_end + right_end))
    roots_found.append(1.0)
    return [(root_value + 1.0) / 2.0 for root_value in roots_found]


def collocation_matrix(node_count):
    points = radau_points(node_count)
    node_table = [[0.0] * node_count for row_number in range(node_count)]
    for column in range(node_count):
        coeffs = [1.0]
        for another in range(node_count):
            if another != column:
                spacing = points[column] - points[another]
                raised = [0.0] + coeffs
                lowered = [entry * points[another] for entry in coeffs] + [0.0]
                coeffs = [
                    (first_entry - second_entry) / spacing
                    for first_entry, second_entry in zip(raised, lowered)
                ]
        integral = [0.0] + [
            entry / (exponent_index + 1) for exponent_index, entry in enumerate(coeffs)
        ]
        for row_number in range(node_count):
            running = 0.0
            for exponent_index in range(len(integral) - 1, -1, -1):
                running = running * points[row_number] + integral[exponent_index]
            node_table[row_number][column] = running
    return node_table


def sine_matrix(count):
    index = np.arange(1, count + 1)
    return math.sqrt(2.0 / (count + 1)) * np.sin(np.pi * np.outer(index, index) / (count + 1))


def eigenvalues(count):
    return 2.0 * np.cos(np.pi * np.arange(1, count + 1) / (count + 1))


def tables():
    coll = np.array(collocation_matrix(NODES))
    sx, sy, sz = (sine_matrix(n) for n in (GX, GY, NZ))
    lam_z, lam_x, lam_y = (eigenvalues(n) for n in (NZ, GX, GY))
    kx = np.einsum("pcx,fg->cpfgx", sx.reshape(16, 2, GX), np.eye(8)).reshape(2, 128, 256)
    n = np.arange(STEPS)
    real_dft = np.zeros((8, 2, STEPS))
    for q in range(8):
        real_dft[q, 0] = np.cos(2 * np.pi * q * n / STEPS)
        real_dft[q, 1] = -np.sin(2 * np.pi * q * n / STEPS) if q else np.cos(np.pi * n)
    shifted = np.zeros_like(real_dft)
    shifted[:, :, :-1] = real_dft[:, :, 1:]
    split = real_dft.reshape(8, 2, 8, 2)
    shifted = shifted.reshape(8, 2, 8, 2)
    nodes = np.eye(NODES).reshape(NODES, 2, 2)
    last = np.zeros((NODES, 2, 2))
    last[:, 1, 1] = 1.0
    two = np.eye(2)
    form = "qrsn,mtj,zw->qrmzstnjw"
    m0 = np.zeros((128, 2, 128))
    m1 = np.zeros((128, 2, 128))
    m0[:, 0] = -np.einsum(form, split, nodes, two).reshape(128, 128)
    m0[:, 1] = np.einsum(form, split, coll.reshape(NODES, 2, 2), two).reshape(128, 128)
    m1[:, 0] = np.einsum(form, shifted, last, two).reshape(128, 128)
    m0, m1 = m0.reshape(128, 256), m1.reshape(128, 256)
    mi = np.einsum("qrsn,mtj,zw->stnjwqrmz", split, nodes, two).reshape(128, 128)
    zf = np.einsum("mn,ksz->mksnz", np.eye(4), sz.reshape(NZ, 32, 2)).reshape(256, 256)
    lam_xy = lam_x.reshape(16, 2).T[:, :, None, None] + lam_y
    lam_xy = np.broadcast_to(lam_xy, (2, 16, 8, 256)).reshape(2, 128, 256)
    lam_zy = lam_z[None, :, None] + lam_y.reshape(2, 1, 128)
    lam_x = np.broadcast_to(lam_x[:, None, None], (GX, 8, 128))
    start = np.linalg.solve(coll, np.ones(NODES))
    exact = dict(lam_xy=lam_xy, m0=m0, m1=m1, mi=mi, lam_zy=lam_zy, lam_x=lam_x)
    arrays = dict(sy=halves(sy), kx=halves(kx))
    arrays.update({k: np.asarray(v, np.float32) for k, v in exact.items()})
    kt = kx.transpose(0, 2, 1)
    arrays.update(zf=halves(zf), zt=halves(zf.T), kt=halves(kt))
    return coll, start, arrays


def halves(matrix):
    matrix = np.asarray(matrix, np.float32)
    upper = matrix.astype(ml_dtypes.bfloat16)
    lower = (matrix - upper.astype(np.float32)).astype(ml_dtypes.bfloat16)
    return np.stack([upper, lower])


COLL, START, TABLES = tables()
NAMES = tuple(TABLES)


def parts(x):
    upper = x.astype(jnp.bfloat16)
    return upper, (x - upper.astype(jnp.float32)).astype(jnp.bfloat16)


def dot3(a, b):
    one = lambda x, y: jnp.dot(x, y, preferred_element_type=jnp.float32)
    return one(a[0], b[0]) + (one(a[0], b[1]) + one(a[1], b[0]))


def horner_tables(q, params, coef, tab, lam):
    partner = (16 - q) % 16 + 8 * ((8 - q) // 8)
    own = params[2 * (q // 2)] + params[2 * (q // 2) + 1]
    mate = params[2 * (partner // 2)] + params[2 * (partner // 2) + 1]
    row = lax.broadcasted_iota(jnp.int32, (8, 128), 0)
    odd = q % 2 == 1
    own = jnp.where(odd, pltpu.roll(own, 4, 0), own)
    mate = jnp.where(odd, mate, pltpu.roll(mate, 4, 0))
    x = jnp.where(row < 4, own, mate)
    bre, bim, mre, mim, dre, dim = [x if c == 0 else pltpu.roll(x, 128 - 16 * c, 1) for c in range(6)]
    pre, pim = bre * mre - bim * mim, bre * mim + bim * mre
    scale = 6.0 * DIFFUSION - REACTION
    ere, eim = 1.0 + scale * dre, scale * dim
    mag = ere * ere + eim * eim
    gre, gim = ere / mag, -eim / mag
    are, aim = DIFFUSION * dre, DIFFUSION * dim
    rre, rim = are * gre - aim * gim, are * gim + aim * gre
    first = q == 0
    for power in range(SWEEPS):
        tre, tim = pre * gre - pim * gim, pre * gim + pim * gre
        gre, gim = gre * rre - gim * rim, gre * rim + gim * rre
        kre, kim = (jnp.sum(v[0:4], axis=0, keepdims=True) for v in (tre, tim))
        ore, oim = (jnp.sum(v[4:8], axis=0, keepdims=True) for v in (tre, tim))
        both = kre + ore
        coef[0, power : power + 1, :] = jnp.where(first, kre, both)
        coef[1, power : power + 1, :] = jnp.where(first, 0.0, kim - oim)
        coef[2, power : power + 1, :] = jnp.where(first, ore, both)

    def entry(e, carry):
        following = []
        for a, c in enumerate(carry):
            col = jnp.broadcast_to(c[:, 0:1], (8, 128))
            acc = jnp.broadcast_to(col[SWEEPS - 1 : SWEEPS], (64, 128))
            for power in range(SWEEPS - 2, -1, -1):
                acc = acc * lam + col[power : power + 1]
            tab[a, e] = acc
            following.append(pltpu.roll(c, 127, 1))
        return tuple(following)

    lax.fori_loop(0, 16, entry, (coef[0], coef[1], coef[2]))


def pack_params(node, mix, back, shifts, out):
    row = lax.broadcasted_iota(jnp.int32, (8, 128), 0)
    lane = lax.broadcasted_iota(jnp.int32, (8, 128), 1)
    kind, i, j = lane // 16, (lane // 4) % 4, lane % 4
    k, m = row // 4, row % 4
    acc = jnp.zeros((8, 128), jnp.float32)
    for c in range(2):
        for kk in range(2):
            here = k == kk
            for l in range(2):
                mine = 2 * node + l
                at_mix = here & (kind == 2 + c) & (m == mine)
                at_back = here & (kind == c) & (i == mine)
                for n in range(4):
                    acc = jnp.where(at_mix & (j == n), mix[c, kk, l, n], acc)
                    acc = jnp.where(at_back & (m == n), back[c, kk, l, n], acc)
                acc = jnp.where(here & (kind == 4 + c) & (m == mine), shifts[c, kk, l], acc)
    out[...] = acc


def kernel(u_hbm, init_hbm, alpha_hbm, mix_hbm, back_hbm, shifts_hbm, *refs):
    consts = dict(zip(NAMES, refs[: len(NAMES)]))
    refs = refs[len(NAMES) :]
    out_u, out_r = refs[:2]
    refs = refs[2:]
    held = dict(zip(NAMES, refs[: len(NAMES)]))
    refs = refs[len(NAMES) :]
    (u_ref, init_ref, su, sf, r1, sp, rp, s2, r2, s3, r3, s4, r4, halo, grid, ub, wb, wedge, whalo, before, coef, tab,
     mm, mb, sw, ow, alpha_ref, mix_ref, back_ref, shifts_ref, heard, load_sem, send_sem, recv_sem) = refs
    step, node, space = (lax.axis_index(a) for a in ("step", "node", "space"))
    me = step * 2 + node
    q, half, chunk = (space % 16) // 2, space % 2, (space // 16 + space) % 2

    load_u = pltpu.make_async_copy(u_hbm, u_ref, load_sem.at[len(NAMES)])
    load_init = pltpu.make_async_copy(init_hbm, init_ref, load_sem.at[len(NAMES) + 1])
    load_u.start()
    loads = {}
    for index, name in enumerate(NAMES):
        loads[name] = pltpu.make_async_copy(consts[name], held[name], load_sem.at[index])
    loads["sy"].start()
    loads["kx"].start()
    small = [
        pltpu.make_async_copy(src, dst, load_sem.at[len(NAMES) + 2 + i])
        for i, (src, dst) in enumerate(
            [(alpha_hbm, alpha_ref), (mix_hbm, mix_ref), (back_hbm, back_ref), (shifts_hbm, shifts_ref)])
    ]
    def get(name):
        loads[name].wait()
        return held[name]

    barrier = pltpu.get_barrier_semaphore()

    def group_id(d):
        other = (me + d) % 16
        return other, {"step": other // 2, "node": other % 2}

    def greet_group(d, _):
        pl.semaphore_signal(barrier, inc=1, device_id=group_id(d)[1])
        return 0

    def near(d):
        return {"space": (space + d) % 32}

    lax.fori_loop(1, 16, greet_group, 0, unroll=True)
    for d in (1, 31):
        pl.semaphore_signal(barrier, inc=1, device_id=near(d))

    def tell(turn):
        for d in (1 << turn, 32 - (1 << turn)):
            pl.semaphore_signal(heard.at[turn], inc=1, device_id=near(d))

    def hear(turn):
        pl.semaphore_wait(heard.at[turn], 2)

    load_u.wait()
    get("sy"), get("kx")
    sy = (held["sy"][0], held["sy"][1])

    def to_sines(field):
        return parts(dot3(parts(field), sy))

    def x_sines(c, rows):
        return dot3((held["kx"][0, c], held["kx"][1, c]), rows)

    rows = to_sines(u_ref[...].reshape(256, 256))
    for c in range(2):
        su[c] = x_sines(c, rows).reshape(16, 8, 256)
    load_init.start()
    for copy in small:
        copy.start()
    for name in NAMES[2:]:
        loads[name].start()
    pl.semaphore_wait(barrier, 17)
    tell(0)

    def remote(src, dst, sem, device, recv=None):
        recv = sem if recv is None else recv
        return pltpu.make_async_remote_copy(
            src_ref=src, dst_ref=dst, send_sem=send_sem.at[sem], recv_sem=recv_sem.at[recv], device_id=device
        )

    up, down = {"space": (space + 1) % 32}, {"space": (space + 31) % 32}
    HALO_UP, HALO_DOWN, PARAMS, SPACE, W_UP, W_DOWN, BEFORE = range(7)
    OTHER, FIELD, FORCE, BACK, CORR = 8, 10, 12, 14, 18
    pending = [
        remote(u_hbm.at[:, 1], halo.at[0], HALO_UP, up),
        remote(u_hbm.at[:, 0], halo.at[1], HALO_DOWN, down),
    ]
    not_first, not_last = space > 0, space < 31

    @pl.when(not_last)
    def _():
        pending[0].start()

    @pl.when(not_first)
    def _():
        pending[1].start()

    @pl.when(space == 0)
    def _():
        halo[0] = jnp.zeros((4, 32, 256), jnp.float32)

    @pl.when(space == 31)
    def _():
        halo[1] = jnp.zeros((4, 32, 256), jnp.float32)

    def to_group(src, dst, sem):
        def body(d, _):
            other, device = group_id(d)
            remote(src.at[other], dst.at[me], sem, device).start()
            return 0

        lax.fori_loop(1, 16, body, 0, unroll=True)
        dst[me] = src[me]

    def block_of(ref, count):
        return ref.at[pl.ds(0, count)]

    def arrived(ref, sem, count):
        part = block_of(ref, count)
        remote(part, part, sem, up).wait_recv()

    def sent(ref, sem, count):
        part = block_of(ref, count)
        remote(part, part, sem, up).wait_send()

    for c in range(2):
        to_group(su.at[c], r1.at[c, 0], FIELD + c)
    hear(0)
    tell(1)

    for copy in small:
        copy.wait()
    pack_params(node, mix_ref, back_ref, shifts_ref, sp)

    def send_params(d, _):
        remote(sp, rp.at[me], PARAMS, group_id(d)[1]).start()
        return 0

    rate = alpha_ref[0].astype(jnp.float32) * (math.log(2.0) / 16.0 / STEPS)
    col = lax.broadcasted_iota(jnp.int32, (1, 256), 1) % 128
    when = (2 * (col // 16) + (col // 4) % 2).astype(jnp.float32)
    scaled = get("m0")[...] * jnp.exp(-rate * when) + get("m1")[...] * jnp.exp(-rate * (when + 1.0))
    mm[0], mm[1] = parts(scaled)
    row = lax.broadcasted_iota(jnp.int32, (128, 128), 0)
    when = (2 * (row // 16) + (row // 4) % 2).astype(jnp.float32)
    mb[0], mb[1] = parts(get("mi")[...] * (jnp.exp(rate * when) * (1.0 / STEPS)))

    lax.fori_loop(1, 16, send_params, 0, unroll=True)
    rp[me] = sp[...]

    begin = [
        jnp.where(step == 0, jnp.where(node == 0, START[m], START[2 + m]), 0.0).astype(jnp.float32) for m in range(2)
    ]
    load_init.wait()
    get("lam_xy")
    hear(1)
    tell(2)

    @pl.when(not_first)
    def _():
        pending[0].wait_recv()

    @pl.when(not_last)
    def _():
        pending[1].wait_recv()

    for nm in range(4):
        for z in range(2):
            u = u_ref[nm, z]
            beside = DIFFUSION * u_ref[nm, 1 - z] + DIFFUSION * halo[z, nm]
            value = beside - (6.0 * DIFFUSION - REACTION) * u - REACTION * (u * u * u)
            if nm < 2:
                value = value + begin[nm] * init_ref[z]
            grid[nm * 2 + z] = value
    rows = to_sines(grid[...].reshape(256, 256))
    for c in range(2):
        value = x_sines(c, rows) + DIFFUSION * held["lam_xy"][c] * su[c].reshape(128, 256)
        sf[c] = value.reshape(16, 8, 256)
        to_group(sf.at[c], r1.at[c, 1], FORCE + c)
        if c == 0:
            hear(2)
            tell(3)

    for c in range(2):
        arrived(r1.at[c, 0], FIELD + c, 15)
        arrived(r1.at[c, 1], FORCE + c, 15)
        spec = dot3((mm[0], mm[1]), parts(r1[c].reshape(256, 256))).reshape(8, 2, 8, 256)
        for h in range(2):
            for part in range(2):
                s2[c, h, :, :, part * 128 : part * 128 + 128] = spec[:, part, :, h * 128 : h * 128 + 128]
        if c == 0:
            hear(3)
        for h in range(2):
            def send_spec(d, _):
                other = (q + d) % 8
                place = (h + c) % 2 * 16 + 2 * other + h
                @pl.when(place != space)
                def _():
                    remote(s2.at[c, h, other], r2.at[space], SPACE, {"space": place}).start()
                return 0

            lax.fori_loop(0, 8, send_spec, 0, unroll=True)
    r2[space] = s2[chunk, half, q]
    other_u = [
        remote(u_hbm.at[pl.ds(2 * i, 2)], ub.at[node, pl.ds(2 * i, 2)], OTHER + i, {"node": 1 - node}) for i in range(2)
    ]
    ub[node] = u_ref[...]

    arrived(rp, PARAMS, 15)
    lam = get("lam_zy")[half] + jnp.broadcast_to(get("lam_x")[2 * me + chunk][0:1], (64, 128))
    horner_tables(q, rp, coef, tab, lam)
    get("zf"), get("zt")
    other_u[0].start()
    other_u[1].start()
    arrived(r2, SPACE, 31)
    sw[...] = dot3((held["zf"][0], held["zf"][1]), parts(r2[...].reshape(256, 256))).reshape(4, 64, 256)

    def solve(z, _):
        at = pl.ds(pl.multiple_of(z * 8, 8), 8)
        re_in = [sw[i, at, 0:128] for i in range(4)]
        im_in = [sw[i, at, 128:256] for i in range(4)]
        for i in range(4):
            re = im = None
            for j in range(4):
                a, e, d = (tab[c, 4 * i + j, at, :] for c in range(3))
                tre, tim = a * re_in[j] - e * im_in[j], e * re_in[j] + d * im_in[j]
                re, im = (tre, tim) if re is None else (re + tre, im + tim)
            ow[i, at, 0:128] = re
            ow[i, at, 128:256] = im
        return 0

    lax.fori_loop(0, 8, solve, 0)
    value = dot3((held["zt"][0], held["zt"][1]), parts(ow[...].reshape(256, 256))).reshape(32, 8, 256)
    for part in range(2):
        s3[:, part] = value[:, :, part * 128 : part * 128 + 128]

    def send_back(d, _):
        other = (space + d) % 32
        remote(s3.at[other], r3.at[chunk, half, q], BACK, {"space": other}, BACK + 2 * chunk + half).start()
        return 0

    lax.fori_loop(1, 32, send_back, 0, unroll=True)
    r3[chunk, half, q] = s3[space]
    get("kt")
    for c in range(2):
        for h in range(2):
            mine = (chunk == c) & (half == h)
            turn = 2 * c + h

            @pl.when(mine)
            def _():
                part = block_of(s3, 7)
                remote(part, part, BACK, up, BACK + turn).wait_recv()

            @pl.when(jnp.logical_not(mine))
            def _():
                part = block_of(s3, 8)
                remote(part, part, BACK, up, BACK + turn).wait_recv()

            lanes = pl.ds(h * 128, 128)
            value = dot3((mb[0], mb[1]), parts(r3[c, h].reshape(128, 128)))
            s4[c, :, :, :, h * 128 : h * 128 + 128] = value.reshape(8, 2, 8, 128)

            def send_corr(d, _):
                other, device = group_id(d)
                remote(s4.at[c, other // 2, :, :, lanes], r4.at[c, :, me, :, lanes], CORR + turn, device).start()
                return 0

            lax.fori_loop(1, 16, send_corr, 0, unroll=True)
        r4[c, :, me] = s4[c, step]
    for copy in other_u:
        copy.wait_recv()
    for c in range(2):
        for h in range(2):
            whole = r4.at[c, :, pl.ds(0, 15), :, pl.ds(h * 128, 128)]
            remote(whole, whole, CORR + 2 * c + h, up).wait_recv()
        for g in range(2):
            rows = to_sines(r4[c, g].reshape(128, 256))
            d = dot3((held["kt"][0, c], held["kt"][1, c]), rows)
            ub[g] = ub[g] + d.reshape(4, 2, 32, 256)

    weight = [
        [jnp.where(node == 0, COLL[m][j], COLL[2 + m][j]).astype(jnp.float32) for j in range(4)] for m in range(2)
    ]

    def nodes_at(n, z):
        return [ub[j // 2, 2 * n + j % 2, z] for j in range(4)]

    seam_up, seam_down = (space % 16) // 15, (space + 15) % 16 // 15
    above = {"space": (space + 1) % 32, "node": (node + seam_up) % 2}
    below = {"space": (space + 31) % 32, "node": (node + seam_down) % 2}
    target = [(node + seam_down) % 2, (node + seam_up) % 2]
    for n in range(2):
        for z in range(2):
            u = nodes_at(n, z)
            for m in range(2):
                rows = [jnp.where(target[z] == 0, COLL[m][j], COLL[2 + m][j]).astype(jnp.float32) for j in range(4)]
                wedge[z, 2 * n + m] = sum(rows[j] * u[j] for j in range(4))
    last = [
        remote(wedge.at[1], whalo.at[0], W_UP, above),
        remote(wedge.at[0], whalo.at[1], W_DOWN, below),
        remote(ub.at[1, 3], before, BEFORE, {"step": (step + 1) % 8}),
    ]
    for copy in last:
        copy.start()
    out_u[...] = ub[node] - u_ref[...]
    for n in range(2):
        for z in range(2):
            u = nodes_at(n, z)
            for m in range(2):
                wb[2 * n + m, z] = sum(weight[m][j] * u[j] for j in range(4))
    x = lax.broadcasted_iota(jnp.int32, (32, 256), 0)
    y = lax.broadcasted_iota(jnp.int32, (32, 256), 1)
    for n in range(2):
        for z in range(2):
            cubes = [v * v * v for v in nodes_at(n, z)]
            for m in range(2):
                w = wb[2 * n + m, z]
                beside = (
                    wb[2 * n + m, 1 - z]
                    + jnp.where(x == 0, 0.0, pltpu.roll(w, 1, 0))
                    + jnp.where(x == 31, 0.0, pltpu.roll(w, 31, 0))
                    + jnp.where(y == 0, 0.0, pltpu.roll(w, 1, 1))
                    + jnp.where(y == 255, 0.0, pltpu.roll(w, 255, 1))
                )
                value = DIFFUSION * beside - (6.0 * DIFFUSION - REACTION) * w
                value = value - REACTION * sum(weight[m][j] * cubes[j] for j in range(4))
                if n == 1:
                    value = value + ub[1, 1, z]
                out_r[2 * n + m, z] = value
    for copy in last:
        copy.wait_recv()
    low = jnp.where(space == 0, 0.0, DIFFUSION)
    high = jnp.where(space == 31, 0.0, DIFFUSION)
    for z in range(2):
        opening = jnp.where(step == 0, init_ref[z], before[z])
        for nm in range(4):
            edge = (low if z == 0 else high) * whalo[z, nm]
            out_r[nm, z] = out_r[nm, z] + (edge + opening if nm < 2 else edge)

    @pl.when(not_last)
    def _():
        pending[0].wait_send()

    @pl.when(not_first)
    def _():
        pending[1].wait_send()

    for copy in last + other_u:
        copy.wait_send()
    for c in range(2):
        sent(su.at[c], FIELD + c, 15)
        sent(sf.at[c], FORCE + c, 15)
        for h in range(2):
            whole = r4.at[c, :, pl.ds(0, 15), :, pl.ds(h * 128, 128)]
            remote(whole, whole, CORR + 2 * c + h, up).wait_send()
    sent(rp, PARAMS, 15)
    sent(r2, SPACE, 31)
    sent(s3, BACK, 31)


def on_device(iterate, initial_value, alpha_power, node_mix, node_back, shifts):
    consts = [jnp.asarray(TABLES[name]) for name in NAMES]
    f32 = jnp.float32
    vmem = lambda *shape: pltpu.VMEM(shape, f32)
    block = jax.ShapeDtypeStruct((4, 2, 32, 256), f32)
    in_vmem, in_any = (pl.BlockSpec(memory_space=m) for m in (pltpu.VMEM, pltpu.HBM))
    correction, rest = pl.pallas_call(
        kernel,
        out_shape=(block, block),
        in_specs=[in_any] * (6 + len(NAMES)),
        out_specs=(in_vmem, in_vmem),
        scratch_shapes=[pltpu.VMEM(TABLES[name].shape, TABLES[name].dtype) for name in NAMES]
        + [vmem(4, 2, 32, 256), vmem(2, 32, 256)]
        + [vmem(2, 16, 8, 256)] * 2
        + [vmem(2, 2, 16, 8, 256)]
        + [vmem(8, 128), vmem(16, 8, 128)]
        + [vmem(2, 2, 8, 8, 256), vmem(32, 8, 256)]
        + [vmem(32, 2, 8, 128), vmem(2, 2, 8, 2, 8, 128)]
        + [vmem(2, 8, 2, 8, 256), vmem(2, 2, 16, 8, 256)]
        + [vmem(2, 4, 32, 256), vmem(8, 32, 256)]
        + [vmem(2, 4, 2, 32, 256), vmem(4, 2, 32, 256)]
        + [vmem(2, 4, 32, 256)] * 2 + [vmem(2, 32, 256)]
        + [vmem(3, 8, 128), vmem(3, 16, 64, 128)]
        + [pltpu.VMEM((2, 128, 256), jnp.bfloat16), pltpu.VMEM((2, 128, 128), jnp.bfloat16)]
        + [vmem(4, 64, 256)] * 2
        + [pltpu.SMEM((1,), jnp.int32), pltpu.SMEM((2, 2, 2, 4), f32), pltpu.SMEM((2, 2, 2, 4), f32), pltpu.SMEM((2, 2, 2), f32)]
        + [pltpu.SemaphoreType.REGULAR((4,))]
        + [pltpu.SemaphoreType.DMA((len(NAMES) + 6,)), pltpu.SemaphoreType.DMA((22,)), pltpu.SemaphoreType.DMA((22,))],
        compiler_params=pltpu.CompilerParams(
            collective_id=0, has_side_effects=True, vmem_limit_bytes=63 * 1024 * 1024
        ),
    )(iterate.reshape(4, 2, 32, 256), initial_value, alpha_power, node_mix, node_back, shifts, *consts)
    updated = iterate + correction.reshape(iterate.shape)
    return updated, rest.reshape(iterate.shape) - updated


def solution(mesh):
    in_specs = (
        P("step", "node", "space", None, None),
        P("space", None, None),
        P(),
        P(None, "step", "node", None),
        P(None, "step", "node", None),
        P(None, "step", "node"),
    )
    out_specs = (P("step", "node", "space", None, None), P("step", "node", "space", None, None))
    return jax.shard_map(
        on_device, mesh=mesh, in_specs=in_specs, out_specs=out_specs, check_vma=False
    )
```
